128 devices in a mesh: outer: 8 (over x_hi, y), inner: 16 (over x_lo, z, core).
Axes of the slice: x: 4 (x_hi: 2, x_lo: 2; x = x_hi * 2 + x_lo), y: 4, z: 4, core: 2. Of those that a mesh axis runs over, the one named last changes fastest.
Arguments:
- image_features: bfloat16 [16384, 1024], P(('outer', 'inner')), may hold values from -40 to 40
- text_features: bfloat16 [16384, 768], P(('outer', 'inner')), may hold values from -40 to 40
- image_projection: bfloat16 [1024, 768], replicated, may hold values from -2 to 2
- text_projection: bfloat16 [768, 768], replicated, may hold values from -2 to 2
Outputs:
- total_loss: float32 [], replicated
- image_grad: bfloat16 [16384, 1024], P(('outer', 'inner'))
- text_grad: bfloat16 [16384, 768], P(('outer', 'inner'))
- image_projection_grad: float32 [1024, 768], replicated
- text_projection_grad: float32 [768, 768], replicated
The draws below stay inside these ranges and needn't reach their ends.
All inputs are finite; a program needn't handle non-finite values.
Results may differ from the reference program's by a relative error of at most 0.02.
Values may be sent and summed in bfloat16 or wider, within the bound.
No kernel may reach another device: no remote copies, remote signals or barrier semaphores. Data moves between devices by JAX's collectives and lax.ppermute only.
A program may use at most 192 MiB of HBM per device.

```python
import jax
import jax.numpy as jnp
from jax import lax

EMBED = 768
VISION = 1024
TEXT_WIDTH = 768
PAIRS = 16384


def shared_latent(key):
    center_key, pair_key, member_key, common_key = jax.random.split(key, 4)
    groups = max(PAIRS // 4, 1)
    member = jax.random.randint(member_key, (PAIRS,), 0, groups)
    centers = jax.random.normal(center_key, (groups, EMBED), jnp.float32)
    pair_part = jax.random.normal(pair_key, (PAIRS, EMBED), jnp.float32)
    common = jax.random.normal(common_key, (1, EMBED), jnp.float32)
    return (centers[member], pair_part, common)


def draw_image_features(key, part):
    cluster, pair_part, common = shared_latent(key)
    key = jax.random.fold_in(key, 11)
    jitter_key, remainder_key = jax.random.split(key, 2)
    jitter = jax.random.normal(jitter_key, (PAIRS, EMBED), jnp.float32)
    remainder = jax.random.normal(remainder_key, (PAIRS, VISION - EMBED), jnp.float32)
    leading = 0.883 * common + 0.281 * cluster + 0.105 * pair_part + 0.361 * jitter
    combined = jnp.concatenate([leading, remainder], axis=1)
    return jnp.clip(combined, -40.0, 40.0).astype(jnp.bfloat16)


def draw_text_features(key, part):
    cluster, pair_part, common = shared_latent(key)
    key = jax.random.fold_in(key, 12)
    jitter_key, remainder_key = jax.random.split(key, 2)
    jitter = jax.random.normal(jitter_key, (PAIRS, EMBED), jnp.float32)
    remainder = jax.random.normal(remainder_key, (PAIRS, TEXT_WIDTH - EMBED), jnp.float32)
    leading = 0.883 * common + 0.281 * cluster + 0.105 * pair_part + 0.361 * jitter
    combined = jnp.concatenate([leading, remainder], axis=1)
    return jnp.clip(combined, -40.0, 40.0).astype(jnp.bfloat16)


def draw_image_projection(key, part):
    key = jax.random.fold_in(key, 21)
    random_part = jnp.clip(jax.random.normal(key, (VISION, EMBED), jnp.float32), -6.0, 6.0)
    return (jnp.eye(VISION, EMBED, dtype=jnp.float32) + 0.5 * VISION ** (-0.5) * random_part).astype(jnp.bfloat16)


def draw_text_projection(key, part):
    key = jax.random.fold_in(key, 22)
    random_part = jnp.clip(jax.random.normal(key, (TEXT_WIDTH, EMBED), jnp.float32), -6.0, 6.0)
    return (jnp.eye(TEXT_WIDTH, EMBED, dtype=jnp.float32) + 0.5 * TEXT_WIDTH ** (-0.5) * random_part).astype(jnp.bfloat16)


def setup_inputs(seed: int = 0) -> dict:
    key_list = jax.random.split(jax.random.key(seed), 5)
    image_features = draw_image_features(jax.random.fold_in(key_list[4], 71), 0)
    text_features = draw_text_features(jax.random.fold_in(key_list[4], 71), 0)
    image_projection = draw_image_projection(jax.random.fold_in(key_list[4], 71), 0)
    text_projection = draw_text_projection(jax.random.fold_in(key_list[4], 71), 0)
    return {"image_features": image_features, "text_features": text_features, "image_projection": image_projection, "text_projection": text_projection}


sharpness_factor = 100.0
norm_eps = 1e-06

def normalize_rows(features, weight):
    projected = jnp.dot(features, weight, preferred_element_type=jnp.float32)
    radius = jnp.sqrt(lax.optimization_barrier(jnp.sum(projected * projected, axis=1, keepdims=True)) + norm_eps)
    return (projected / radius, radius)

def back_rows(unit_rows, radius, emb_grad, features, weight):
    along = lax.optimization_barrier(jnp.sum(unit_rows * emb_grad, axis=1, keepdims=True))
    projected_grad = ((emb_grad - unit_rows * along) / radius).astype(jnp.bfloat16)
    feature_grad = jnp.dot(projected_grad, weight.T, preferred_element_type=jnp.float32).astype(jnp.bfloat16)
    weight_grad = jnp.dot(features.T, projected_grad, preferred_element_type=jnp.float32)
    return (feature_grad, weight_grad)

def reference(image_features, text_features, image_projection, text_projection):
    image_unit, image_radius = normalize_rows(image_features, image_projection)
    text_unit, text_radius = normalize_rows(text_features, text_projection)
    picture_latent_vector = image_unit.astype(jnp.bfloat16)
    caption_latent_vector = text_unit.astype(jnp.bfloat16)
    affinity_matrix = sharpness_factor * jnp.dot(picture_latent_vector, caption_latent_vector.T, preferred_element_type=jnp.float32)
    paired_diagonal_entries = sharpness_factor * lax.optimization_barrier(jnp.sum(picture_latent_vector.astype(jnp.float32) * caption_latent_vector.astype(jnp.float32), axis=1))
    centered_affinity_matrix = jnp.exp(affinity_matrix - sharpness_factor)
    picture_axis_normalizer = jnp.log(lax.optimization_barrier(jnp.sum(centered_affinity_matrix, axis=1))) + sharpness_factor
    caption_axis_normalizer = jnp.log(lax.optimization_barrier(jnp.sum(centered_affinity_matrix, axis=0))) + sharpness_factor
    total_loss = (jnp.sum(picture_axis_normalizer - paired_diagonal_entries) + jnp.sum(caption_axis_normalizer - paired_diagonal_entries)) / (2.0 * PAIRS)
    normalized_probabilities = (0.5 * sharpness_factor * (jnp.exp(affinity_matrix - picture_axis_normalizer[:, None]) + jnp.exp(affinity_matrix - caption_axis_normalizer[None, :]))).astype(jnp.bfloat16)
    picture_latent_adjoint = jnp.dot(normalized_probabilities, caption_latent_vector, preferred_element_type=jnp.float32) - sharpness_factor * caption_latent_vector.astype(jnp.float32)
    caption_latent_adjoint = jnp.dot(normalized_probabilities.T, picture_latent_vector, preferred_element_type=jnp.float32) - sharpness_factor * picture_latent_vector.astype(jnp.float32)
    image_grad, image_projection_grad = back_rows(image_unit, image_radius, picture_latent_adjoint, image_features, image_projection)
    text_grad, text_projection_grad = back_rows(text_unit, text_radius, caption_latent_adjoint, text_features, text_projection)
    return (total_loss, image_grad, text_grad, image_projection_grad, text_projection_grad)
```

```python
import jax
import jax.numpy as jnp
from jax import lax
from jax.sharding import Mesh, PartitionSpec as P

sharpness_factor = 100.0
norm_eps = 1e-06
X = ("xh", "xl")
YZ = ("y", "z")
XYZ = ("xh", "xl", "y", "z")
ALL = ("xh", "y", "xl", "z", "c")
f32 = jnp.float32
bf16 = jnp.bfloat16


def normalize_rows(features, weight):
    projected = jnp.dot(features, weight, preferred_element_type=f32)
    radius = jnp.sqrt(jnp.sum(projected * projected, axis=1, keepdims=True) + norm_eps)
    return (projected / radius, radius)


def back_rows(unit_rows, radius, emb_grad, features, weight):
    along = jnp.sum(unit_rows * emb_grad, axis=1, keepdims=True)
    projected_grad = ((emb_grad - unit_rows * along) / radius).astype(bf16)
    feature_grad = lax.dot_general(
        projected_grad, weight, (((1,), (1,)), ((), ())), preferred_element_type=f32
    ).astype(bf16)
    weight_grad = lax.dot_general(
        features, projected_grad, (((0,), (0,)), ((), ())), preferred_element_type=f32
    )
    return (feature_grad, weight_grad)


def from_x(v, k):
    return lax.ppermute(v, X, [(i, (i - k) % 4) for i in range(4)])


def from_core(v):
    return lax.ppermute(v, "c", [(0, 1), (1, 0)])


def spread(v, axes, n):
    return lax.all_to_all(jnp.broadcast_to(v[None], (n,) + v.shape), axes, 0, 0)


def gather_text(t):
    half = t.shape[0] // 2
    up = from_x(t, 1)
    down = from_x(t, 3)
    far = jnp.concatenate([from_x(up[:half], 1), from_x(down[half:], 3)], axis=0)
    mine = jnp.concatenate([t, up, far, down], axis=0)
    return jnp.concatenate([mine, from_core(mine)], axis=0)


def column_totals(part):
    n = part.shape[0] // 2
    both = part[:n] + from_core(part[n:]), part[n:] + from_core(part[:n])
    both = jnp.stack(both).reshape(2, 4, n // 4)
    total = both
    for k in (1, 3, 2):
        total = total + jnp.roll(from_x(both, k), k, axis=1)
    return total.reshape(-1)


def scatter_text(g):
    n = g.shape[0] // 2
    b = n // 4
    h = b // 2
    g = g[:n] + from_core(g[n:].astype(bf16)).astype(f32)
    g0, g1, g2, g3 = (g[k * b : (k + 1) * b] for k in range(4))
    low = from_x(g2[:h].astype(bf16), 3).astype(f32)
    high = from_x(g2[h:].astype(bf16), 1).astype(f32)
    g1 = jnp.concatenate([g1[:h] + low, g1[h:]], axis=0)
    g3 = jnp.concatenate([g3[:h], g3[h:] + high], axis=0)
    return g0 + from_x(g1.astype(bf16), 3).astype(f32) + from_x(g3.astype(bf16), 1).astype(f32)


def reduce_weights(image_term, text_term, loss_part):
    rows = image_term.shape[0] + text_term.shape[0]
    core = lax.axis_index("c")
    both = jnp.concatenate([image_term, text_term], axis=0)
    width = both.shape[1]
    half = rows // 2
    both = both.reshape(2, half, width)
    mine = lax.dynamic_index_in_dim(both, core, 0, keepdims=False)
    other = lax.dynamic_index_in_dim(both, 1 - core, 0, keepdims=False)
    mine = mine + from_core(other.astype(bf16)).astype(f32)
    hi = loss_part.astype(bf16)
    lo = (loss_part - hi.astype(f32)).astype(bf16)
    n = 64
    each = half // n
    tail = jnp.zeros((16 - each, width), bf16).at[0, 0].set(hi).at[0, 1].set(lo)
    sent = jnp.concatenate(
        [mine.astype(bf16).reshape(n, each, width), jnp.broadcast_to(tail[None], (n,) + tail.shape)],
        axis=1,
    )
    got = jnp.sum(lax.all_to_all(sent, XYZ, 0, 0).astype(f32), axis=0)
    loss = got[each, 0] + got[each, 1]
    loss = loss + from_core(loss)
    full = spread(got[:each].astype(bf16), XYZ, n).reshape(half, width)
    swapped = from_core(full)
    out = jnp.zeros((2, half, width), bf16)
    out = lax.dynamic_update_index_in_dim(out, full, core, 0)
    out = lax.dynamic_update_index_in_dim(out, swapped, 1 - core, 0)
    out = out.reshape(rows, width).astype(f32)
    return out[: image_term.shape[0]], out[image_term.shape[0] :], loss


def body(image_features, text_features, image_projection, text_projection):
    image_unit, image_radius = normalize_rows(image_features, image_projection)
    text_unit, text_radius = normalize_rows(text_features, text_projection)
    image_emb = image_unit.astype(bf16)
    text_emb = text_unit.astype(bf16)
    own, width = image_emb.shape
    place = lax.axis_index(YZ)
    images = spread(image_emb, YZ, 16).reshape(16 * own, width)
    texts = gather_text(text_emb)
    logits = sharpness_factor * lax.dot_general(
        images, texts, (((1,), (1,)), ((), ())), preferred_element_type=f32
    )
    matched = sharpness_factor * jnp.sum(image_emb.astype(f32) * text_emb.astype(f32), axis=1)
    centered = jnp.exp(logits - sharpness_factor)
    row_total = jnp.sum(spread(jnp.sum(centered, axis=1), YZ, 16), axis=0)
    column_total = column_totals(jnp.sum(centered, axis=0))
    row_lse = jnp.log(row_total) + sharpness_factor
    column_lse = jnp.log(column_total) + sharpness_factor
    own_rows = lax.dynamic_slice_in_dim(row_lse, place * own, own)
    loss_part = jnp.sum(own_rows + column_lse[:own] - 2.0 * matched)
    weights = (
        0.5
        * sharpness_factor
        * (jnp.exp(logits - row_lse[:, None]) + jnp.exp(logits - column_lse[None, :]))
    ).astype(bf16)
    image_part = jnp.dot(weights, texts, preferred_element_type=f32).reshape(16, own, width)
    text_part = lax.dot_general(
        weights, images, (((0,), (0,)), ((), ())), preferred_element_type=f32
    )
    here = (jnp.arange(16) == place)[:, None, None]
    image_part = image_part - jnp.where(here, sharpness_factor * text_emb.astype(f32)[None], 0.0)
    image_emb_grad = jnp.sum(
        lax.all_to_all(image_part.astype(bf16), YZ, 0, 0).astype(f32), axis=0
    )
    text_part = jnp.concatenate(
        [text_part[:own] - sharpness_factor * image_emb.astype(f32), text_part[own:]], axis=0
    )
    text_emb_grad = scatter_text(text_part)
    image_grad, image_term = back_rows(
        image_unit, image_radius, image_emb_grad, image_features, image_projection
    )
    text_grad, text_term = back_rows(
        text_unit, text_radius, text_emb_grad, text_features, text_projection
    )
    image_projection_grad, text_projection_grad, loss = reduce_weights(
        image_term, text_term, loss_part
    )
    pairs = own * 128
    return (
        loss / (2.0 * pairs),
        image_grad,
        text_grad,
        image_projection_grad,
        text_projection_grad,
    )


def solution(mesh):
    grid = Mesh(mesh.devices.reshape(2, 4, 2, 4, 2), ALL)
    rows = P(ALL, None)
    return jax.shard_map(
        body,
        mesh=grid,
        in_specs=(rows, rows, P(), P()),
        out_specs=(P(), rows, rows, P(), P()),
        check_vma=False,
    )
```

```python
import jax
import jax.numpy as jnp
from jax import lax
from jax.experimental import pallas as pl
from jax.experimental.pallas import tpu as pltpu
from jax.sharding import Mesh, PartitionSpec as P

sharpness_factor = 100.0
norm_eps = 1e-06
X = ("xh", "xl")
YZ = ("y", "z")
XYZ = ("xh", "xl", "y", "z")
ALL = ("xh", "y", "xl", "z", "c")
TILE = 256
f32 = jnp.float32
bf16 = jnp.bfloat16


def normalize_rows(features, weight):
    projected = jnp.dot(features, weight, preferred_element_type=f32)
    radius = jnp.sqrt(jnp.sum(projected * projected, axis=1, keepdims=True) + norm_eps)
    return (projected / radius, radius)


def from_x(v, k):
    return lax.ppermute(v, X, [(i, (i - k) % 4) for i in range(4)])


def from_core(v):
    return lax.ppermute(v, "c", [(0, 1), (1, 0)])


def spread(v, axes, n):
    return lax.all_to_all(jnp.broadcast_to(v[None], (n,) + v.shape), axes, 0, 0)


def gather_text(t):
    half = t.shape[0] // 2
    up = from_x(t, 1)
    down = from_x(t, 3)
    far = jnp.concatenate([from_x(up[:half], 1), from_x(down[half:], 3)], axis=0)
    mine = jnp.concatenate([t, up, far, down], axis=0)
    return jnp.concatenate([mine, from_core(mine)], axis=0)


def column_totals(part):
    n = part.shape[0] // 2
    both = part[:n] + from_core(part[n:]), part[n:] + from_core(part[:n])
    both = jnp.stack(both).reshape(2, 4, n // 4)
    total = both
    for k in (1, 3, 2):
        total = total + jnp.roll(from_x(both, k), k, axis=1)
    return total.reshape(-1)


def scatter_text(g):
    n = g.shape[0] // 2
    b = n // 4
    h = b // 2
    g = g[:n] + from_core(g[n:].astype(bf16)).astype(f32)
    g0, g1, g2, g3 = (g[k * b : (k + 1) * b] for k in range(4))
    low = from_x(g2[:h].astype(bf16), 3).astype(f32)
    high = from_x(g2[h:].astype(bf16), 1).astype(f32)
    g1 = jnp.concatenate([g1[:h] + low, g1[h:]], axis=0)
    g3 = jnp.concatenate([g3[:h], g3[h:] + high], axis=0)
    return g0 + from_x(g1.astype(bf16), 3).astype(f32) + from_x(g3.astype(bf16), 1).astype(f32)


def params():
    return pltpu.CompilerParams(vmem_limit_bytes=40 * 1024 * 1024)

def turned(row):
    return jnp.broadcast_to(row, (128, row.shape[1])).T


def logits_kernel(images, texts, logits, row_sum, column_sum):
    value = sharpness_factor * lax.dot_general(
        images[...], texts[...], (((1,), (1,)), ((), ())), preferred_element_type=f32
    )
    logits[...] = value
    e = jnp.exp(value - sharpness_factor)
    rows, columns = e.shape
    by_lane = e[:, :128]
    for k in range(1, columns // 128):
        by_lane = by_lane + e[:, k * 128 : (k + 1) * 128]
    row_sum[...] = jnp.sum(by_lane.T, axis=0, keepdims=True)
    by_column = jnp.sum(e, axis=0, keepdims=True)

    @pl.when(pl.program_id(0) == 0)
    def _():
        column_sum[...] = by_column

    @pl.when(pl.program_id(0) > 0)
    def _():
        column_sum[...] += by_column


def block_logits(images, texts):
    n, width = images.shape
    m = texts.shape[0]
    return pl.pallas_call(
        logits_kernel,
        grid=(n // TILE,),
        in_specs=[
            pl.BlockSpec((TILE, width), lambda i: (i, 0)),
            pl.BlockSpec((m, width), lambda i: (0, 0)),
        ],
        out_specs=[
            pl.BlockSpec((TILE, m), lambda i: (i, 0)),
            pl.BlockSpec((1, TILE), lambda i: (0, i)),
            pl.BlockSpec((1, m), lambda i: (0, 0)),
        ],
        out_shape=[
            jax.ShapeDtypeStruct((n, m), f32),
            jax.ShapeDtypeStruct((1, n), f32),
            jax.ShapeDtypeStruct((1, m), f32),
        ],
        compiler_params=params(),
        cost_estimate=pl.CostEstimate(
            flops=2 * n * m * width, bytes_accessed=4 * n * m + 2 * (n + m) * width, transcendentals=n * m
        ),
        name="block_logits",
    )(images, texts)


def weights_kernel(place, logits, row_parts, column_parts, texts, weights, grad):
    row_lse = jnp.log(jnp.sum(row_parts[...], axis=0, keepdims=True)) + sharpness_factor
    column_lse = jnp.log(jnp.sum(column_parts[...], axis=0, keepdims=True)) + sharpness_factor
    value = logits[...]
    rows, columns = value.shape
    row_lse = jnp.concatenate([turned(row_lse)] * (columns // 128), axis=1)
    w = (
        0.5 * sharpness_factor * (jnp.exp(value - row_lse) + jnp.exp(value - column_lse))
    ).astype(bf16)
    weights[...] = w
    part = jnp.dot(w, texts[...], preferred_element_type=f32)
    i = pl.program_id(0)
    per = rows // 128
    for k in range(per):
        here = jnp.where(place[0] == i * per + k, sharpness_factor, 0.0)
        grad[k * 128 : (k + 1) * 128, :] = (
            part[k * 128 : (k + 1) * 128] - here * texts[:128, :].astype(f32)
        ).astype(bf16)


def block_weights(place, logits, row_parts, column_parts, texts):
    n, m = logits.shape
    width = texts.shape[1]
    return pl.pallas_call(
        weights_kernel,
        grid=(n // TILE,),
        in_specs=[
            pl.BlockSpec(memory_space=pltpu.SMEM),
            pl.BlockSpec((TILE, m), lambda i: (i, 0)),
            pl.BlockSpec((row_parts.shape[0], TILE), lambda i: (0, i)),
            pl.BlockSpec(column_parts.shape, lambda i: (0, 0)),
            pl.BlockSpec((m, width), lambda i: (0, 0)),
        ],
        out_specs=[
            pl.BlockSpec((TILE, m), lambda i: (i, 0)),
            pl.BlockSpec((TILE, width), lambda i: (i, 0)),
        ],
        out_shape=[
            jax.ShapeDtypeStruct((n, m), bf16),
            jax.ShapeDtypeStruct((n, width), bf16),
        ],
        compiler_params=params(),
        cost_estimate=pl.CostEstimate(
            flops=2 * n * m * width,
            bytes_accessed=6 * n * m + 2 * (n + m) * width,
            transcendentals=2 * n * m,
        ),
        name="block_weights",
    )(place, logits, row_parts, column_parts, texts)


def text_kernel(weights, images, own, grad):
    part = lax.dot_general(
        weights[...], images[...], (((0,), (0,)), ((), ())), preferred_element_type=f32
    )
    i = pl.program_id(0)
    here = jnp.where(i == 0, sharpness_factor, 0.0)
    grad[128:, :] = part[128:]
    grad[:128, :] = part[:128] - here * own[...].astype(f32)


def block_text_grad(weights, images, own):
    n, m = weights.shape
    width = images.shape[1]
    return pl.pallas_call(
        text_kernel,
        grid=(m // TILE,),
        in_specs=[
            pl.BlockSpec((n, TILE), lambda i: (0, i)),
            pl.BlockSpec((n, width), lambda i: (0, 0)),
            pl.BlockSpec(own.shape, lambda i: (0, 0)),
        ],
        out_specs=pl.BlockSpec((TILE, width), lambda i: (i, 0)),
        out_shape=jax.ShapeDtypeStruct((m, width), f32),
        compiler_params=params(),
        cost_estimate=pl.CostEstimate(
            flops=2 * n * m * width, bytes_accessed=2 * n * m + 2 * n * width + 4 * m * width, transcendentals=0
        ),
        name="block_text_grad",
    )(weights, images, own)


def other_half(v, core):
    n = v.shape[1] // 2
    mine = lax.dynamic_slice_in_dim(v, core * n, n, axis=1)
    away = lax.dynamic_slice_in_dim(v, (1 - core) * n, n, axis=1)
    return jnp.concatenate([mine, from_core(away)], axis=0)


def back_rows(unit_rows, radius, emb_grad):
    along = jnp.sum(unit_rows * emb_grad, axis=1, keepdims=True)
    return ((emb_grad - unit_rows * along) / radius).astype(bf16)


def feature_grad(projected_grad, weight):
    return lax.dot_general(
        projected_grad, weight, (((1,), (1,)), ((), ())), preferred_element_type=f32
    ).astype(bf16)


def weight_grad(features, projected_grad):
    return lax.dot_general(
        features, projected_grad, (((0,), (0,)), ((), ())), preferred_element_type=f32
    )


def reduce_weights(image_term, text_term, loss_part, core):
    n = 64
    width = image_term.shape[1]
    image_blocks = image_term.astype(bf16).reshape(n, 8, width)
    text_blocks = text_term.astype(bf16).reshape(-1, 8, width)
    used = text_blocks.shape[0]
    hi = loss_part.astype(bf16)
    lo = (loss_part - hi.astype(f32)).astype(bf16)
    lanes = jnp.arange(width)
    extra = jnp.where(lanes == 0, hi, jnp.where(lanes == 1, lo, jnp.zeros((), bf16)))
    extra = jnp.broadcast_to(extra, (n - used, 8, width))
    sent = jnp.concatenate(
        [image_blocks, jnp.concatenate([text_blocks, extra], axis=0)], axis=1
    )
    got = jnp.sum(lax.all_to_all(sent, XYZ, 0, 0).astype(f32), axis=0)
    high = got.astype(bf16)
    low = jnp.broadcast_to((got[:, 0:1] + got[:, 1:2]), got.shape)
    low = (low - low.astype(bf16).astype(f32)).astype(bf16)
    total = (got[:, 0:1] + got[:, 1:2]).astype(bf16)
    row = lax.broadcasted_iota(jnp.int32, got.shape, 0)
    lane = lax.broadcasted_iota(jnp.int32, got.shape, 1)
    carries = (lax.axis_index(XYZ) >= used) & (row >= 8)
    block = jnp.where(carries, jnp.where(lane == 0, total, low), high)
    full = spread(block, XYZ, n)
    swapped = from_core(full)
    first = core == 0

    def whole(a, b):
        a, b = a.reshape(-1, width).astype(f32), b.reshape(-1, width).astype(f32)
        return jnp.concatenate([jnp.where(first, a, b), jnp.where(first, b, a)], axis=0)

    image = whole(full[:, :8], swapped[:, :8])
    text = whole(full[:used, 8:], swapped[:used, 8:])
    loss = full[n - 1, 8, :2].astype(f32) + swapped[n - 1, 8, :2].astype(f32)
    return image, text, loss[0] + loss[1]


def body(image_features, text_features, image_projection, text_projection):
    core = lax.axis_index("c")
    place = lax.axis_index(YZ)
    image_unit, image_radius = normalize_rows(image_features, image_projection)
    image_emb = image_unit.astype(bf16)
    own, width = image_emb.shape
    images = spread(image_emb, YZ, 16).reshape(16 * own, width)
    text_unit, text_radius = normalize_rows(text_features, text_projection)
    text_emb = text_unit.astype(bf16)
    texts = gather_text(text_emb)
    image_halves = other_half(image_features, core)
    text_halves = other_half(text_features, core)
    logits, row_part, column_part = block_logits(images, texts)
    matched = sharpness_factor * jnp.sum(image_emb.astype(f32) * text_emb.astype(f32), axis=1)
    row_parts = spread(row_part, YZ, 16).reshape(16, -1)
    column_total = column_totals(column_part.reshape(-1)).reshape(1, -1)
    weights, image_part = block_weights(
        place.reshape(1), logits, row_parts, column_total, texts
    )
    own_rows = jnp.sum(lax.dynamic_slice_in_dim(row_parts, place * own, own, axis=1), axis=0)
    loss_part = jnp.sum(
        jnp.log(own_rows)
        + jnp.log(column_total[0, :own])
        + 2.0 * (sharpness_factor - matched)
    )
    image_emb_grad = jnp.sum(
        lax.all_to_all(image_part.reshape(16, own, width), YZ, 0, 0).astype(f32), axis=0
    )
    text_part = block_text_grad(weights, images, image_emb)
    text_emb_grad = scatter_text(text_part)
    text_back = back_rows(text_unit, text_radius, text_emb_grad)
    image_back = back_rows(image_unit, image_radius, image_emb_grad)
    text_both = jnp.concatenate([text_back, from_core(text_back)], axis=0)
    image_both = jnp.concatenate([image_back, from_core(image_back)], axis=0)
    text_term = weight_grad(text_halves, text_both)
    image_term = weight_grad(image_halves, image_both)
    image_projection_grad, text_projection_grad, loss = reduce_weights(
        image_term, text_term, loss_part, core
    )
    pairs = own * 128
    return (
        loss / (2.0 * pairs),
        feature_grad(image_back, image_projection),
        feature_grad(text_back, text_projection),
        image_projection_grad,
        text_projection_grad,
    )


def solution(mesh):
    grid = Mesh(mesh.devices.reshape(2, 4, 2, 4, 2), ALL)
    rows = P(ALL, None)
    return jax.shard_map(
        body,
        mesh=grid,
        in_specs=(rows, rows, P(), P()),
        out_specs=(P(), rows, rows, P(), P()),
        check_vma=False,
    )
```

```python
import jax
import jax.numpy as jnp
from jax import lax
from jax.experimental import pallas as pl
from jax.experimental.pallas import tpu as pltpu
from jax.sharding import Mesh, PartitionSpec as P

sharpness_factor = 100.0
norm_eps = 1e-06
X = ("xh", "xl")
PAIR_Z = ("xl", "z")
PAIR_YZ = ("xl", "y", "z")
PAIR_ZC = ("xl", "z", "c")
ALL = ("xh", "y", "xl", "z", "c")
TILE = 512
LTILE = 512
f32 = jnp.float32
bf16 = jnp.bfloat16


def normalize_rows(features, weight):
    projected = jnp.dot(features, weight, preferred_element_type=f32)
    radius = jnp.sqrt(jnp.sum(projected * projected, axis=1, keepdims=True) + norm_eps)
    return (projected / radius, radius)


def from_core(v):
    return lax.ppermute(v, "c", [(0, 1), (1, 0)])


def from_mirror(v):
    return lax.ppermute(v, X, [(i, 3 - i) for i in range(4)])


def from_y(v, k):
    return lax.ppermute(v, "y", [(i, (i - k) % 4) for i in range(4)])


def spread(v, axes, n):
    return lax.all_to_all(jnp.broadcast_to(v[None], (n,) + v.shape), axes, 0, 0)


def gather_text(t):
    n = t.shape[0]
    pair = jnp.concatenate([t, from_mirror(t)], axis=0)
    up = from_y(pair, 1)
    down = from_y(pair, 3)
    far = [from_y(up[:n], 1), from_y(down[n:], 3)]
    return jnp.concatenate([pair, up] + far + [down], axis=0)


def column_totals(part):
    part = part.reshape(4, 2, -1)
    part = part + from_mirror(part)[:, ::-1]
    total = part
    for k in (1, 3, 2):
        total = total + jnp.roll(from_y(part, k), k, axis=0)
    return total.reshape(1, -1)


def plus(*parts):
    return sum(p.astype(f32) for p in parts)


def scatter_text(g):
    b = g.shape[0] // 4
    h = b // 2
    g0, g1, g2, g3 = (g[k * b : (k + 1) * b] for k in range(4))
    low = from_y(g2[:h], 3)
    high = from_y(g2[h:], 1)
    g1 = jnp.concatenate([plus(g1[:h], low).astype(bf16), g1[h:]], axis=0)
    g3 = jnp.concatenate([g3[:h], plus(g3[h:], high).astype(bf16)], axis=0)
    g0 = plus(g0, from_y(g1, 3), from_y(g3, 1))
    return g0[:h] + from_mirror(g0[h:].astype(bf16)).astype(f32)


def params():
    return pltpu.CompilerParams(vmem_limit_bytes=40 * 1024 * 1024)


def logits_kernel(images, texts, logits, row_sum, column_sum):
    value = sharpness_factor * lax.dot_general(
        images[...], texts[...], (((1,), (1,)), ((), ())), preferred_element_type=f32
    )
    logits[...] = value
    e = jnp.exp(value - sharpness_factor)
    by_lane = e[:, :128]
    for k in range(1, e.shape[1] // 128):
        by_lane = by_lane + e[:, k * 128 : (k + 1) * 128]
    row_sum[...] = jnp.sum(by_lane.T, axis=0, keepdims=True)
    by_column = jnp.sum(e, axis=0, keepdims=True)

    @pl.when(pl.program_id(0) == 0)
    def _():
        column_sum[...] = by_column

    @pl.when(pl.program_id(0) > 0)
    def _():
        column_sum[...] += by_column


def block_logits(images, texts):
    n, width = images.shape
    m = texts.shape[0]
    return pl.pallas_call(
        logits_kernel,
        grid=(n // LTILE,),
        in_specs=[
            pl.BlockSpec((LTILE, width), lambda i: (i, 0)),
            pl.BlockSpec((m, width), lambda i: (0, 0)),
        ],
        out_specs=[
            pl.BlockSpec((LTILE, m), lambda i: (i, 0)),
            pl.BlockSpec((1, LTILE), lambda i: (0, i)),
            pl.BlockSpec((1, m), lambda i: (0, 0)),
        ],
        out_shape=[
            jax.ShapeDtypeStruct((n, m), f32),
            jax.ShapeDtypeStruct((1, n), f32),
            jax.ShapeDtypeStruct((1, m), f32),
        ],
        compiler_params=params(),
        cost_estimate=pl.CostEstimate(
            flops=2 * n * m * width, bytes_accessed=4 * n * m + 2 * (n + m) * width, transcendentals=n * m
        ),
        name="block_logits",
    )(images, texts)


def grads_kernel(place, logits, row_parts, column_parts, images, texts, own, image_part, text_part, total):
    i = pl.program_id(0)
    row_lse = jnp.log(jnp.sum(row_parts[...], axis=0, keepdims=True)) + sharpness_factor
    column_lse = jnp.log(jnp.sum(column_parts[...], axis=0, keepdims=True)) + sharpness_factor
    value = logits[...]
    rows, columns = value.shape
    by_row = jnp.broadcast_to(row_lse, (128, rows)).T
    by_row = jnp.concatenate([by_row] * (columns // 128), axis=1)
    weights = (
        0.5 * sharpness_factor * (jnp.exp(value - by_row) + jnp.exp(value - column_lse))
    ).astype(bf16)
    part = jnp.dot(weights, texts[...], preferred_element_type=f32)
    per = rows // 128
    for k in range(per):
        here = jnp.where(place[0] == i * per + k, sharpness_factor, 0.0)
        image_part[k * 128 : (k + 1) * 128, :] = (
            part[k * 128 : (k + 1) * 128] - here * texts[:128, :].astype(f32)
        ).astype(bf16)
    share = lax.dot_general(
        weights, images[...], (((0,), (0,)), ((), ())), preferred_element_type=f32
    )

    @pl.when(i == 0)
    def _():
        total[...] = share

    @pl.when(i > 0)
    def _():
        total[...] += share

    @pl.when(i == pl.num_programs(0) - 1)
    def _():
        text_part[:128, :] = (total[:128, :] - sharpness_factor * own[...].astype(f32)).astype(bf16)
        text_part[128:, :] = total[128:, :].astype(bf16)


def block_grads(place, logits, row_parts, column_parts, images, texts, own):
    n, m = logits.shape
    width = texts.shape[1]
    return pl.pallas_call(
        grads_kernel,
        grid=(n // TILE,),
        in_specs=[
            pl.BlockSpec(memory_space=pltpu.SMEM),
            pl.BlockSpec((TILE, m), lambda i: (i, 0)),
            pl.BlockSpec((row_parts.shape[0], TILE), lambda i: (0, i)),
            pl.BlockSpec(column_parts.shape, lambda i: (0, 0)),
            pl.BlockSpec((TILE, width), lambda i: (i, 0)),
            pl.BlockSpec((m, width), lambda i: (0, 0)),
            pl.BlockSpec(own.shape, lambda i: (0, 0)),
        ],
        out_specs=[
            pl.BlockSpec((TILE, width), lambda i: (i, 0)),
            pl.BlockSpec((m, width), lambda i: (0, 0)),
        ],
        out_shape=[
            jax.ShapeDtypeStruct((n, width), bf16),
            jax.ShapeDtypeStruct((m, width), bf16),
        ],
        scratch_shapes=[pltpu.VMEM((m, width), f32)],
        compiler_params=params(),
        cost_estimate=pl.CostEstimate(
            flops=4 * n * m * width,
            bytes_accessed=4 * n * m + 4 * (n + m) * width,
            transcendentals=2 * n * m,
        ),
        name="block_grads",
    )(place, logits, row_parts, column_parts, images, texts, own)


def whole_kernel(core, mine, other, image, text):
    h = pl.program_id(0)
    n, rows, width = mine.shape
    half = rows // 2
    used = text.shape[0] // half

    def put(src):
        image[...] = src[:, :half].astype(f32).reshape(image.shape)
        text[...] = src[:used, half:].astype(f32).reshape(text.shape)

    @pl.when(h == core[0])
    def _():
        put(mine)

    @pl.when(h != core[0])
    def _():
        put(other)


def whole_terms(core, mine, other, used):
    n, rows, width = mine.shape
    half = rows // 2
    block = pl.BlockSpec(mine.shape, lambda h: (0, 0, 0))
    return pl.pallas_call(
        whole_kernel,
        grid=(2,),
        in_specs=[pl.BlockSpec(memory_space=pltpu.SMEM), block, block],
        out_specs=[
            pl.BlockSpec((n * half, width), lambda h: (h, 0)),
            pl.BlockSpec((used * half, width), lambda h: (h, 0)),
        ],
        out_shape=[
            jax.ShapeDtypeStruct((2 * n * half, width), f32),
            jax.ShapeDtypeStruct((2 * used * half, width), f32),
        ],
        compiler_params=params(),
        cost_estimate=pl.CostEstimate(flops=0, bytes_accessed=8 * n * rows * width, transcendentals=0),
        name="whole_terms",
    )(core, mine, other)


def other_half(v, core):
    n = v.shape[1] // 2
    mine = lax.dynamic_slice_in_dim(v, core * n, n, axis=1)
    away = lax.dynamic_slice_in_dim(v, (1 - core) * n, n, axis=1)
    return jnp.concatenate([mine, from_core(away)], axis=0)


def back_rows(unit_rows, radius, emb_grad):
    along = jnp.sum(unit_rows * emb_grad, axis=1, keepdims=True)
    return ((emb_grad - unit_rows * along) / radius).astype(bf16)


def feature_grad(projected_grad, weight):
    return lax.dot_general(
        projected_grad, weight, (((1,), (1,)), ((), ())), preferred_element_type=f32
    ).astype(bf16)


def weight_grad(features, projected_grad):
    return lax.dot_general(
        features, projected_grad, (((0,), (0,)), ((), ())), preferred_element_type=f32
    )


def reduce_weights(image_term, text_term, loss_part, core):
    n = 32
    rows = 16
    width = image_term.shape[1]
    image_blocks = image_term.astype(bf16).reshape(n, rows, width)
    text_blocks = text_term.astype(bf16).reshape(-1, rows, width)
    used = text_blocks.shape[0]
    lane = lax.broadcasted_iota(jnp.int32, (rows, width), 1)

    def split(v):
        high = v.astype(bf16)
        low = (v - high.astype(f32)).astype(bf16)
        return jnp.where(lane == 0, high, jnp.where(lane == 1, low, jnp.zeros((), bf16)))

    extra = jnp.broadcast_to(split(loss_part), (n - used, rows, width))
    sent = jnp.concatenate(
        [image_blocks, jnp.concatenate([text_blocks, extra], axis=0)], axis=1
    )
    got = jnp.sum(lax.all_to_all(sent, PAIR_YZ, 0, 0).astype(f32), axis=0)
    total = got[rows : rows + 1, 0:1] + got[rows : rows + 1, 1:2]
    block = jnp.concatenate(
        [
            got[:rows].astype(bf16),
            jnp.where(lax.axis_index(PAIR_YZ) >= used, split(total), got[rows:].astype(bf16)),
        ],
        axis=0,
    )
    block = plus(block, lax.ppermute(block, "xh", [(0, 1), (1, 0)]))
    total = block[rows : rows + 1, 0:1] + block[rows : rows + 1, 1:2]
    block = jnp.concatenate(
        [
            block[:rows].astype(bf16),
            jnp.where(lax.axis_index(PAIR_YZ) >= used, split(total), block[rows:].astype(bf16)),
        ],
        axis=0,
    )
    full = spread(block, PAIR_YZ, n)
    swapped = from_core(full)
    image, text = whole_terms(core.reshape(1), full, swapped, used)
    loss = plus(full[n - 1, rows, :2], swapped[n - 1, rows, :2])
    return image, text, loss[0] + loss[1]


def body(image_features, text_features, image_projection, text_projection):
    core = lax.axis_index("c")
    place = lax.axis_index(PAIR_Z)
    image_unit, image_radius = normalize_rows(image_features, image_projection)
    image_emb = image_unit.astype(bf16)
    own, width = image_emb.shape
    images = spread(image_emb, PAIR_Z, 8).reshape(8 * own, width)
    text_unit, text_radius = normalize_rows(text_features, text_projection)
    text_emb = text_unit.astype(bf16)
    image_halves = other_half(image_features, core)
    text_halves = other_half(text_features, core)
    images, texts, image_halves, text_halves = lax.optimization_barrier(
        (images, gather_text(text_emb), image_halves, text_halves)
    )
    rows = images.shape[0]
    images = jnp.concatenate([images, from_core(images)], axis=0)
    logits, row_part, column_part = block_logits(images, texts)
    row_flip = jnp.concatenate([row_part[:, rows:], row_part[:, :rows]], axis=1)
    first = core == 0
    row_pair = jnp.stack(
        [jnp.where(first, row_part[0], row_flip[0]), jnp.where(first, row_flip[0], row_part[0])]
    )
    row_parts = lax.all_to_all(
        jnp.broadcast_to(row_pair[None], (8, 2, 2 * rows)).reshape(16, 1, 2 * rows), PAIR_ZC, 0, 0
    ).reshape(16, -1)
    column_total = column_totals(column_part)
    image_parts, text_part = block_grads(
        place.reshape(1), logits, row_parts, column_total, images, texts, image_emb
    )
    other_part = from_core(image_parts[rows:])
    image_part = plus(image_parts[:rows], other_part).astype(bf16)
    image_emb_grad = jnp.sum(
        lax.all_to_all(image_part.reshape(8, own, width), PAIR_Z, 0, 0).astype(f32), axis=0
    )
    text_emb_grad = scatter_text(text_part)
    matched = sharpness_factor * jnp.sum(image_emb.astype(f32) * text_emb.astype(f32), axis=1)
    own_rows = jnp.sum(lax.dynamic_slice_in_dim(row_parts, place * own, own, axis=1), axis=0)
    loss_part = jnp.sum(
        jnp.log(own_rows)
        + jnp.log(column_total[0, :own])
        + 2.0 * (sharpness_factor - matched)
    )
    text_back = back_rows(text_unit, text_radius, text_emb_grad)
    image_back = back_rows(image_unit, image_radius, image_emb_grad)
    text_both = jnp.concatenate([text_back, from_core(text_back)], axis=0)
    image_both = jnp.concatenate([image_back, from_core(image_back)], axis=0)
    text_term = weight_grad(text_halves, text_both)
    image_term = weight_grad(image_halves, image_both)
    image_projection_grad, text_projection_grad, loss = reduce_weights(
        image_term, text_term, loss_part, core
    )
    pairs = own * 128
    return (
        loss / (2.0 * pairs),
        feature_grad(image_back, image_projection),
        feature_grad(text_back, text_projection),
        image_projection_grad,
        text_projection_grad,
    )


def solution(mesh):
    grid = Mesh(mesh.devices.reshape(2, 4, 2, 4, 2), ALL)
    rows = P(ALL, None)
    return jax.shard_map(
        body,
        mesh=grid,
        in_specs=(rows, rows, P(), P()),
        out_specs=(P(), rows, rows, P(), P()),
        check_vma=False,
    )
```

```python
import jax
import jax.numpy as jnp
from jax import lax
from jax.experimental import pallas as pl
from jax.experimental.pallas import tpu as pltpu
from jax.sharding import Mesh, PartitionSpec as P

sharpness_factor = 100.0
norm_eps = 1e-06
X = ("xh", "xl")
PAIR_Z = ("xl", "z")
YZ = ("y", "z")
ALL = ("xh", "y", "xl", "z", "c")
TILE = 512
LTILE = 512
GRADS_MIB = 40
f32 = jnp.float32
bf16 = jnp.bfloat16


def normalize_rows(features, weight):
    projected = jnp.dot(features, weight, preferred_element_type=f32)
    radius = jnp.sqrt(jnp.sum(projected * projected, axis=1, keepdims=True) + norm_eps)
    return (projected / radius, radius)


def from_core(v):
    return lax.ppermute(v, "c", [(0, 1), (1, 0)])


def from_mirror(v):
    return lax.ppermute(v, X, [(i, 3 - i) for i in range(4)])


def from_x(v, k):
    return lax.ppermute(v, X, [(i, (i - k) % 4) for i in range(4)])


def from_y(v, k):
    return lax.ppermute(v, "y", [(i, (i - k) % 4) for i in range(4)])


def hbm(v):
    return pltpu.with_memory_space_constraint(v, pltpu.HBM)


def spread(v, axes, n):
    return lax.all_to_all(jnp.broadcast_to(v[None], (n,) + v.shape), axes, 0, 0)


def gather_text(pair):
    n = pair.shape[0] // 2
    up = from_y(pair, 1)
    down = from_y(pair, 3)
    far = [from_y(up[:n], 1), from_y(down[n:], 3)]
    return jnp.concatenate([pair, up] + far + [down], axis=0)


def column_totals(part):
    part = part.reshape(4, 2, -1)
    part = part + from_mirror(part)[:, ::-1]
    total = part
    for k in (1, 3, 2):
        total = total + jnp.roll(from_y(part, k), k, axis=0)
    return total.reshape(1, -1)


def row_totals(part):
    n = part.shape[1] // 2
    other = from_core(part)
    part = part + jnp.concatenate([other[:, n:], other[:, :n]], axis=1)
    part = part + lax.ppermute(part, "xl", [(0, 1), (1, 0)])
    return part + sum(lax.ppermute(part, "z", [(i, (i - k) % 4) for i in range(4)]) for k in (1, 3, 2))


def plus(*parts):
    return sum(p.astype(f32) for p in parts)


def scatter_text(g):
    b = g.shape[0] // 4
    h = b // 2
    g0, g1, g2, g3 = (g[k * b : (k + 1) * b] for k in range(4))
    low = from_y(g2[:h], 3)
    high = from_y(g2[h:], 1)
    g1 = jnp.concatenate([plus(g1[:h], low).astype(bf16), g1[h:]], axis=0)
    g3 = jnp.concatenate([g3[:h], plus(g3[h:], high).astype(bf16)], axis=0)
    g1, g3 = lax.optimization_barrier((g1, g3))
    g0 = plus(g0, from_y(g1, 3), from_y(g3, 1))
    return g0[:h] + from_mirror(g0[h:].astype(bf16)).astype(f32)


def params(mib=40):
    return pltpu.CompilerParams(vmem_limit_bytes=mib * 1024 * 1024)


def logits_kernel(mine, other, texts, logits, row_sum, column_sum):
    i = pl.program_id(0)
    images = jnp.where(i < pl.num_programs(0) // 2, mine[...], other[...])
    value = sharpness_factor * lax.dot_general(
        images, texts[...], (((1,), (1,)), ((), ())), preferred_element_type=f32
    )
    logits[...] = value
    e = jnp.exp(value - sharpness_factor)
    by_lane = e[:, :128]
    for k in range(1, e.shape[1] // 128):
        by_lane = by_lane + e[:, k * 128 : (k + 1) * 128]
    row_sum[...] = jnp.sum(by_lane.T, axis=0, keepdims=True)
    by_column = jnp.sum(e, axis=0, keepdims=True)

    @pl.when(i == 0)
    def _():
        column_sum[...] = by_column

    @pl.when(i > 0)
    def _():
        column_sum[...] += by_column


def block_logits(mine, other, texts):
    n, width = mine.shape
    half = n // LTILE
    n = 2 * n
    m = texts.shape[0]
    return pl.pallas_call(
        logits_kernel,
        grid=(n // LTILE,),
        in_specs=[
            pl.BlockSpec((LTILE, width), lambda i: (jnp.minimum(i, half - 1), 0)),
            pl.BlockSpec((LTILE, width), lambda i: (jnp.maximum(i - half, 0), 0)),
            pl.BlockSpec((m, width), lambda i: (0, 0)),
        ],
        out_specs=[
            pl.BlockSpec((LTILE, m), lambda i: (i, 0)),
            pl.BlockSpec((1, LTILE), lambda i: (0, i)),
            pl.BlockSpec((1, m), lambda i: (0, 0)),
        ],
        out_shape=[
            pltpu.HBM((n, m), f32),
            jax.ShapeDtypeStruct((1, n), f32),
            jax.ShapeDtypeStruct((1, m), f32),
        ],
        compiler_params=params(),
        cost_estimate=pl.CostEstimate(
            flops=2 * n * m * width, bytes_accessed=4 * n * m + 2 * (n + m) * width, transcendentals=n * m
        ),
        name="block_logits",
    )(mine, other, texts)


def grads_kernel(
    place, logits, row_total, column_total, mine, other, texts, own, part_mine, part_other, text_part, total
):
    i = pl.program_id(0)
    half = pl.num_programs(0) // 2
    images = jnp.where(i < half, mine[...], other[...])
    row_lse = jnp.log(row_total[...]) + sharpness_factor
    column_lse = jnp.log(column_total[...]) + sharpness_factor
    value = logits[...]
    rows, columns = value.shape
    by_row = jnp.broadcast_to(row_lse, (128, rows)).T
    by_row = jnp.concatenate([by_row] * (columns // 128), axis=1)
    weights = (
        0.5 * sharpness_factor * (jnp.exp(value - by_row) + jnp.exp(value - column_lse))
    ).astype(bf16)
    part = jnp.dot(weights, texts[...], preferred_element_type=f32)
    per = rows // 128

    @pl.when(i < half)
    def _():
        for k in range(per):
            here = jnp.where(place[0] == i * per + k, sharpness_factor, 0.0)
            part_mine[k * 128 : (k + 1) * 128, :] = (
                part[k * 128 : (k + 1) * 128] - here * texts[:128, :].astype(f32)
            ).astype(bf16)

    @pl.when(i >= half)
    def _():
        part_other[...] = part.astype(bf16)

    share = lax.dot_general(
        weights, images, (((0,), (0,)), ((), ())), preferred_element_type=f32
    )

    @pl.when(i == 0)
    def _():
        total[...] = share

    @pl.when(i > 0)
    def _():
        total[...] += share

    @pl.when(i == pl.num_programs(0) - 1)
    def _():
        text_part[:128, :] = (total[:128, :] - sharpness_factor * own[...].astype(f32)).astype(bf16)
        text_part[128:, :] = total[128:, :].astype(bf16)


def block_grads(place, logits, row_total, column_total, mine, other, texts, own):
    n, m = logits.shape
    width = texts.shape[1]
    half = n // TILE // 2
    first = pl.BlockSpec((TILE, width), lambda i: (jnp.minimum(i, half - 1), 0))
    second = pl.BlockSpec((TILE, width), lambda i: (jnp.maximum(i - half, 0), 0))
    return pl.pallas_call(
        grads_kernel,
        grid=(n // TILE,),
        in_specs=[
            pl.BlockSpec(memory_space=pltpu.SMEM),
            pl.BlockSpec((TILE, m), lambda i: (i, 0)),
            pl.BlockSpec((1, TILE), lambda i: (0, i)),
            pl.BlockSpec((1, m), lambda i: (0, 0)),
            first,
            second,
            pl.BlockSpec((m, width), lambda i: (0, 0)),
            pl.BlockSpec(own.shape, lambda i: (0, 0)),
        ],
        out_specs=[first, second, pl.BlockSpec((m, width), lambda i: (0, 0))],
        out_shape=[
            jax.ShapeDtypeStruct((n // 2, width), bf16),
            jax.ShapeDtypeStruct((n // 2, width), bf16),
            jax.ShapeDtypeStruct((m, width), bf16),
        ],
        scratch_shapes=[pltpu.VMEM((m, width), f32)],
        compiler_params=params(GRADS_MIB),
        cost_estimate=pl.CostEstimate(
            flops=4 * n * m * width,
            bytes_accessed=4 * n * m + 4 * (n + m) * width,
            transcendentals=2 * n * m,
        ),
        name="block_grads",
    )(place, logits, row_total, column_total, mine, other, texts, own)


def whole_kernel(core, mine, other, image, text):
    rows = image.shape[0] // mine.shape[0]

    def put(src):
        image[...] = src[:, :rows].astype(f32).reshape(image.shape)
        text[...] = src[:, rows:].astype(f32).reshape(text.shape)

    @pl.when(pl.program_id(0) == core[0])
    def _():
        put(mine)

    @pl.when(pl.program_id(0) != core[0])
    def _():
        put(other)


def whole_terms(core, mine, other, rows):
    n, both, width = mine.shape
    block = pl.BlockSpec(mine.shape, lambda h: (0, 0, 0))
    return pl.pallas_call(
        whole_kernel,
        grid=(2,),
        in_specs=[pl.BlockSpec(memory_space=pltpu.SMEM), block, block],
        out_specs=[
            pl.BlockSpec((n * rows, width), lambda h: (h, 0)),
            pl.BlockSpec((n * (both - rows), width), lambda h: (h, 0)),
        ],
        out_shape=[
            jax.ShapeDtypeStruct((2 * n * rows, width), f32),
            jax.ShapeDtypeStruct((2 * n * (both - rows), width), f32),
        ],
        compiler_params=params(),
        cost_estimate=pl.CostEstimate(flops=0, bytes_accessed=12 * n * both * width, transcendentals=0),
        name="whole_terms",
    )(core, mine, other)


def other_half(v, core):
    n = v.shape[1] // 2
    mine = lax.dynamic_slice_in_dim(v, core * n, n, axis=1)
    away = lax.dynamic_slice_in_dim(v, (1 - core) * n, n, axis=1)
    return jnp.concatenate([mine, from_core(away)], axis=0)


def back_rows(unit_rows, radius, emb_grad):
    along = jnp.sum(unit_rows * emb_grad, axis=1, keepdims=True)
    return ((emb_grad - unit_rows * along) / radius).astype(bf16)


def feature_grad(projected_grad, weight):
    return lax.dot_general(
        projected_grad, weight, (((1,), (1,)), ((), ())), preferred_element_type=f32
    ).astype(bf16)


def weight_grad(features, projected_grad):
    return lax.dot_general(
        features, projected_grad, (((0,), (0,)), ((), ())), preferred_element_type=f32
    )


def reduce_weights(image_term, text_term, loss_part, core):
    n = 16
    width = image_term.shape[1]
    image_blocks = image_term.astype(bf16).reshape(n, -1, width)
    text_blocks = text_term.astype(bf16).reshape(n, -1, width)
    rows = image_blocks.shape[1]
    both = rows + text_blocks.shape[1]
    lane = lax.broadcasted_iota(jnp.int32, (8, width), 1)

    def split(v):
        high = lax.reduce_precision(v, 8, 7)
        low = (v - high).astype(bf16)
        return jnp.where(lane == 0, high.astype(bf16), jnp.where(lane == 1, low, jnp.zeros((), bf16)))

    extra = jnp.broadcast_to(split(loss_part), (n, 8, width))
    sent = jnp.concatenate([image_blocks, text_blocks, extra], axis=1)
    got = plus(*lax.all_to_all(sent, YZ, 0, 0))
    block = jnp.concatenate(
        [got[:both].astype(bf16), split(got[both:, 0:1] + got[both:, 1:2])], axis=0
    )
    total = plus(block, *(from_x(block, k) for k in (1, 3, 2)))
    loss = total[both, 0] + total[both, 1]
    full = spread(total[:both].astype(bf16), YZ, n)
    image, text = whole_terms(core.reshape(1), full, from_core(full), rows)
    return image, text, loss


def body(image_features, text_features, image_projection, text_projection):
    core = lax.axis_index("c")
    place = lax.axis_index(PAIR_Z)
    text_unit, text_radius = normalize_rows(text_features, text_projection)
    text_emb = text_unit.astype(bf16)
    image_unit, image_radius = normalize_rows(image_features, image_projection)
    image_emb = image_unit.astype(bf16)
    own, width = image_emb.shape
    images = spread(image_emb, PAIR_Z, 8).reshape(8 * own, width)
    pair = jnp.concatenate([text_emb, from_mirror(text_emb)], axis=0)
    pair, later_image, later_text = lax.optimization_barrier((pair, image_features, text_features))
    image_halves = other_half(later_image, core)
    text_halves = other_half(later_text, core)
    images, texts, image_halves, text_halves = lax.optimization_barrier(
        (images, gather_text(pair), image_halves, text_halves)
    )
    images_other = hbm(from_core(images))
    texts = hbm(texts)
    logits, row_part, column_part = block_logits(images, images_other, texts)
    row_total = row_totals(row_part)
    column_total = column_totals(column_part)
    image_part, other_part, text_part = block_grads(
        place.reshape(1), logits, row_total, column_total, images, images_other, texts, image_emb
    )
    image_part = plus(image_part, from_core(other_part)).astype(bf16)
    image_emb_grad = plus(*lax.all_to_all(image_part.reshape(8, own, width), PAIR_Z, 0, 0))
    text_emb_grad = scatter_text(text_part)
    matched = sharpness_factor * jnp.sum(image_emb.astype(f32) * text_emb.astype(f32), axis=1)
    own_rows = lax.dynamic_slice_in_dim(row_total[0], place * own, own)
    loss_part = jnp.sum(
        jnp.log(own_rows)
        + jnp.log(column_total[0, :own])
        + 2.0 * (sharpness_factor - matched)
    )
    loss_part = loss_part + from_core(loss_part)
    text_back = back_rows(text_unit, text_radius, text_emb_grad)
    image_back = back_rows(image_unit, image_radius, image_emb_grad)
    text_both = jnp.concatenate([text_back, from_core(text_back)], axis=0)
    image_both = jnp.concatenate([image_back, from_core(image_back)], axis=0)
    text_term = weight_grad(text_halves, text_both)
    image_term = weight_grad(image_halves, image_both)
    image_projection_grad, text_projection_grad, loss = reduce_weights(
        image_term, text_term, loss_part, core
    )
    pairs = own * 128
    return (
        loss / (2.0 * pairs),
        feature_grad(image_back, image_projection),
        feature_grad(text_back, text_projection),
        image_projection_grad,
        text_projection_grad,
    )


def solution(mesh):
    grid = Mesh(mesh.devices.reshape(2, 4, 2, 4, 2), ALL)
    rows = P(ALL, None)
    return jax.shard_map(
        body,
        mesh=grid,
        in_specs=(rows, rows, P(), P()),
        out_specs=(P(), rows, rows, P(), P()),
        check_vma=False,
    )
```

```python
import math

import jax
import jax.numpy as jnp
from jax import lax
from jax.experimental import pallas as pl
from jax.experimental.pallas import tpu as pltpu
from jax.sharding import Mesh, PartitionSpec as P

sharpness_factor = 100.0
norm_eps = 1e-06
X = ("xh", "xl")
PAIR_Z = ("xl", "z")
YZ = ("y", "z")
ALL = ("xh", "y", "xl", "z", "c")
TILE = 512
LOG2 = sharpness_factor * math.log2(math.e)
f32 = jnp.float32
bf16 = jnp.bfloat16


def normalize_rows(features, weight):
    projected = jnp.dot(features, weight, preferred_element_type=f32)
    radius = jnp.sqrt(jnp.sum(projected * projected, axis=1, keepdims=True) + norm_eps)
    return (projected / radius, radius)


def from_core(v):
    return lax.ppermute(v, "c", [(0, 1), (1, 0)])


def from_mirror(v):
    return lax.ppermute(v, X, [(i, 3 - i) for i in range(4)])


def from_x(v, k):
    return lax.ppermute(v, X, [(i, (i - k) % 4) for i in range(4)])


def from_y(v, k):
    return lax.ppermute(v, "y", [(i, (i - k) % 4) for i in range(4)])


def hbm(v):
    return pltpu.with_memory_space_constraint(v, pltpu.HBM)


def spread(v, axes, n):
    return lax.all_to_all(jnp.broadcast_to(v[None], (n,) + v.shape), axes, 0, 0)


def gather_text(pair):
    n = pair.shape[0] // 2
    up = from_y(pair, 1)
    down = from_y(pair, 3)
    far = [from_y(up[:n], 1), from_y(down[n:], 3)]
    return jnp.concatenate([pair, up] + far + [down], axis=0)


def column_totals(part):
    part = part.reshape(4, 2, -1)
    part = part + from_mirror(part)[:, ::-1]
    total = part
    for k in (1, 3, 2):
        total = total + jnp.roll(from_y(part, k), k, axis=0)
    return total.reshape(1, -1)


def row_totals(part):
    n = part.shape[1] // 2
    flipped = jnp.concatenate([part[:, n:], part[:, :n]], axis=1)

    def from_pair(v, xl, c):
        pairs = [(i, i ^ (2 * xl + c)) for i in range(4)]
        return lax.ppermute(v, ("xl", "c"), pairs)

    part = part + from_pair(part, 1, 0) + from_pair(flipped, 1, 1) + from_pair(flipped, 0, 1)
    return part + sum(lax.ppermute(part, "z", [(i, (i - k) % 4) for i in range(4)]) for k in (1, 3, 2))


def plus(*parts):
    return sum(p.astype(f32) for p in parts)


def scatter_text(g):
    b = g.shape[0] // 4
    h = b // 2
    g0, g1, g2, g3 = (g[k * b : (k + 1) * b] for k in range(4))
    low = from_y(g2[:h], 3)
    high = from_y(g2[h:], 1)
    g1 = jnp.concatenate([plus(g1[:h], low).astype(bf16), g1[h:]], axis=0)
    g3 = jnp.concatenate([g3[:h], plus(g3[h:], high).astype(bf16)], axis=0)
    g1, g3 = lax.optimization_barrier((g1, g3))
    g0 = plus(g0, from_y(g1, 3), from_y(g3, 1))
    return g0[:h] + from_mirror(g0[h:].astype(bf16)).astype(f32)


def params(mib=40):
    return pltpu.CompilerParams(vmem_limit_bytes=mib * 1024 * 1024)


def logits_kernel(mine, other, texts, logits, row_sum, column_sum):
    i = pl.program_id(0)
    images = jnp.where(i < pl.num_programs(0) // 2, mine[...], other[...])
    value = lax.dot_general(
        images, texts[...], (((1,), (1,)), ((), ())), preferred_element_type=f32
    )
    logits[...] = value
    e = jnp.exp2(value * LOG2 - LOG2)
    by_lane = e[:, :128]
    for k in range(1, e.shape[1] // 128):
        by_lane = by_lane + e[:, k * 128 : (k + 1) * 128]
    row_sum[...] = jnp.sum(by_lane.T, axis=0, keepdims=True)
    column_sum[...] = jnp.where(i == 0, 0.0, column_sum[...]) + jnp.sum(e, axis=0, keepdims=True)


def block_logits(mine, other, texts):
    rows, width = mine.shape
    n = 2 * rows
    m = texts.shape[0]
    steps = n // TILE
    half = steps // 2
    return pl.pallas_call(
        logits_kernel,
        grid=(steps,),
        in_specs=[
            pl.BlockSpec((TILE, width), lambda i: (jnp.minimum(i, half - 1), 0)),
            pl.BlockSpec((TILE, width), lambda i: (jnp.maximum(i - half, 0), 0)),
            pl.BlockSpec((m, width), lambda i: (0, 0)),
        ],
        out_specs=[
            pl.BlockSpec((TILE, m), lambda i: (i, 0)),
            pl.BlockSpec((1, TILE), lambda i: (0, i)),
            pl.BlockSpec((1, m), lambda i: (0, 0)),
        ],
        out_shape=[
            pltpu.HBM((n, m), f32),
            jax.ShapeDtypeStruct((1, n), f32),
            jax.ShapeDtypeStruct((1, m), f32),
        ],
        compiler_params=params(),
        cost_estimate=pl.CostEstimate(
            flops=2 * n * m * width, bytes_accessed=4 * n * m + 2 * (n + m) * width, transcendentals=n * m
        ),
        name="block_logits",
    )(mine, other, texts)


def grads_kernel(
    place, logits, row_total, column_total, mine, other, texts, own, part_mine, part_other, text_part, total, last
):
    i = pl.program_id(0)
    half = (pl.num_programs(0) - 1) // 2
    before = jnp.where(i == 0, jnp.zeros((), bf16), last[...])
    images = jnp.where(i <= half, mine[...], other[...])
    part = jnp.dot(before, texts[...], preferred_element_type=f32)
    share = lax.dot_general(
        before, images, (((0,), (0,)), ((), ())), preferred_element_type=f32
    )
    shift = LOG2 - math.log2(0.5 * sharpness_factor)
    value = logits[...] * LOG2
    rows, columns = value.shape
    row_lse = jnp.log2(row_total[...]) + shift
    column_lse = jnp.log2(column_total[...]) + shift
    by_row = jnp.broadcast_to(row_lse, (128, rows)).T
    by_row = jnp.concatenate([by_row] * (columns // 128), axis=1)
    last[...] = (jnp.exp2(value - by_row) + jnp.exp2(value - column_lse)).astype(bf16)
    total[...] = jnp.where(i == 0, 0.0, total[...]) + share
    per = rows // 128

    @pl.when(i <= half)
    def _():
        for k in range(per):
            here = jnp.where(place[0] == (i - 1) * per + k, sharpness_factor, 0.0)
            part_mine[k * 128 : (k + 1) * 128, :] = (
                part[k * 128 : (k + 1) * 128] - here * texts[:128, :].astype(f32)
            ).astype(bf16)

    @pl.when(i > half)
    def _():
        part_other[...] = part.astype(bf16)

    @pl.when(i == pl.num_programs(0) - 1)
    def _():
        text_part[:128, :] = (total[:128, :] - sharpness_factor * own[...].astype(f32)).astype(bf16)
        text_part[128:, :] = total[128:, :].astype(bf16)


def block_grads(place, logits, row_total, column_total, mine, other, texts, own):
    n, m = logits.shape
    width = texts.shape[1]
    steps = n // TILE
    half = steps // 2
    first = pl.BlockSpec((TILE, width), lambda i: (jnp.clip(i - 1, 0, half - 1), 0))
    second = pl.BlockSpec((TILE, width), lambda i: (jnp.clip(i - 1 - half, 0, half - 1), 0))
    return pl.pallas_call(
        grads_kernel,
        grid=(steps + 1,),
        in_specs=[
            pl.BlockSpec(memory_space=pltpu.SMEM),
            pl.BlockSpec((TILE, m), lambda i: (jnp.minimum(i, steps - 1), 0)),
            pl.BlockSpec((1, TILE), lambda i: (0, jnp.minimum(i, steps - 1))),
            pl.BlockSpec((1, m), lambda i: (0, 0)),
            first,
            second,
            pl.BlockSpec((m, width), lambda i: (0, 0)),
            pl.BlockSpec(own.shape, lambda i: (0, 0)),
        ],
        out_specs=[
            first,
            second,
            pl.BlockSpec((m, width), lambda i: (0, 0)),
        ],
        out_shape=[
            jax.ShapeDtypeStruct((n // 2, width), bf16),
            jax.ShapeDtypeStruct((n // 2, width), bf16),
            jax.ShapeDtypeStruct((m, width), bf16),
        ],
        scratch_shapes=[pltpu.VMEM((m, width), f32), pltpu.VMEM((TILE, m), bf16)],
        compiler_params=params(),
        cost_estimate=pl.CostEstimate(
            flops=4 * n * m * width,
            bytes_accessed=4 * n * m + 4 * (n + m) * width,
            transcendentals=2 * n * m,
        ),
        name="block_grads",
    )(place, logits, row_total, column_total, mine, other, texts, own)


def whole_kernel(core, mine, other, image, text):
    rows = image.shape[0] // mine.shape[0]

    def put(src):
        image[...] = src[:, :rows].astype(f32).reshape(image.shape)
        text[...] = src[:, rows:].astype(f32).reshape(text.shape)

    @pl.when(pl.program_id(0) == core[0])
    def _():
        put(mine)

    @pl.when(pl.program_id(0) != core[0])
    def _():
        put(other)


def whole_terms(core, mine, other, rows):
    n, both, width = mine.shape
    block = pl.BlockSpec(mine.shape, lambda h: (0, 0, 0))
    return pl.pallas_call(
        whole_kernel,
        grid=(2,),
        in_specs=[pl.BlockSpec(memory_space=pltpu.SMEM), block, block],
        out_specs=[
            pl.BlockSpec((n * rows, width), lambda h: (h, 0)),
            pl.BlockSpec((n * (both - rows), width), lambda h: (h, 0)),
        ],
        out_shape=[
            jax.ShapeDtypeStruct((2 * n * rows, width), f32),
            jax.ShapeDtypeStruct((2 * n * (both - rows), width), f32),
        ],
        compiler_params=params(),
        cost_estimate=pl.CostEstimate(flops=0, bytes_accessed=12 * n * both * width, transcendentals=0),
        name="whole_terms",
    )(core, mine, other)


def other_half(v, core):
    n = v.shape[1] // 2
    mine = lax.dynamic_slice_in_dim(v, core * n, n, axis=1)
    away = lax.dynamic_slice_in_dim(v, (1 - core) * n, n, axis=1)
    return jnp.concatenate([mine, from_core(away)], axis=0)


def back_rows(unit_rows, radius, emb_grad):
    along = jnp.sum(unit_rows * emb_grad, axis=1, keepdims=True)
    return ((emb_grad - unit_rows * along) / radius).astype(bf16)


def feature_grad(projected_grad, weight):
    return lax.dot_general(
        projected_grad, weight, (((1,), (1,)), ((), ())), preferred_element_type=f32
    ).astype(bf16)


def weight_grad(features, projected_grad):
    return lax.dot_general(
        features, projected_grad, (((0,), (0,)), ((), ())), preferred_element_type=f32
    )


def reduce_weights(image_term, text_term, loss_part, core):
    n = 16
    width = image_term.shape[1]
    image_blocks = image_term.astype(bf16).reshape(n, -1, width)
    text_blocks = text_term.astype(bf16).reshape(n, -1, width)
    rows = image_blocks.shape[1]
    both = rows + text_blocks.shape[1]
    lane = lax.broadcasted_iota(jnp.int32, (8, width), 1)

    def split(v):
        high = lax.reduce_precision(v, 8, 7)
        low = (v - high).astype(bf16)
        return jnp.where(lane == 0, high.astype(bf16), jnp.where(lane == 1, low, jnp.zeros((), bf16)))

    extra = jnp.broadcast_to(split(loss_part), (n, 8, width))
    sent = jnp.concatenate([image_blocks, text_blocks, extra], axis=1)
    got = plus(*lax.all_to_all(sent, YZ, 0, 0))
    block = jnp.concatenate(
        [got[:both].astype(bf16), split(got[both:, 0:1] + got[both:, 1:2])], axis=0
    )
    total = plus(block, *(from_x(block, k) for k in (1, 3, 2)))
    loss = total[both, 0] + total[both, 1]
    full = spread(total[:both].astype(bf16), YZ, n)
    image, text = whole_terms(core.reshape(1), full, from_core(full), rows)
    return image, text, loss


def body(image_features, text_features, image_projection, text_projection):
    core = lax.axis_index("c")
    place = lax.axis_index(PAIR_Z)
    text_unit, text_radius = normalize_rows(text_features, text_projection)
    text_emb = text_unit.astype(bf16)
    image_unit, image_radius = normalize_rows(image_features, image_projection)
    image_emb = image_unit.astype(bf16)
    own, width = image_emb.shape
    images = spread(image_emb, PAIR_Z, 8).reshape(8 * own, width)
    pair = jnp.concatenate([text_emb, from_mirror(text_emb)], axis=0)
    pair, later_image, later_text = lax.optimization_barrier((pair, image_features, text_features))
    image_halves = other_half(later_image, core)
    text_halves = other_half(later_text, core)
    images, texts, image_halves, text_halves = lax.optimization_barrier(
        (images, gather_text(pair), image_halves, text_halves)
    )
    images_other = hbm(from_core(images))
    texts = hbm(texts)
    logits, row_part, column_part = block_logits(images, images_other, texts)
    row_total = row_totals(row_part)
    column_total = column_totals(column_part)
    image_part, other_part, text_part = block_grads(
        place.reshape(1), logits, row_total, column_total, images, images_other, texts, image_emb
    )
    image_part = plus(image_part, from_core(other_part)).astype(bf16)
    image_emb_grad = plus(*lax.all_to_all(image_part.reshape(8, own, width), PAIR_Z, 0, 0))
    text_emb_grad = scatter_text(text_part)
    matched = sharpness_factor * jnp.sum(image_emb.astype(f32) * text_emb.astype(f32), axis=1)
    own_rows = lax.dynamic_slice_in_dim(row_total[0], place * own, own)
    loss_part = jnp.sum(
        jnp.log(own_rows)
        + jnp.log(column_total[0, :own])
        + 2.0 * (sharpness_factor - matched)
    )
    loss_part = loss_part + from_core(loss_part)
    text_back = back_rows(text_unit, text_radius, text_emb_grad)
    image_back = back_rows(image_unit, image_radius, image_emb_grad)
    text_both = jnp.concatenate([text_back, from_core(text_back)], axis=0)
    image_both = jnp.concatenate([image_back, from_core(image_back)], axis=0)
    text_term = weight_grad(text_halves, text_both)
    image_term = weight_grad(image_halves, image_both)
    image_projection_grad, text_projection_grad, loss = reduce_weights(
        image_term, text_term, loss_part, core
    )
    pairs = own * 128
    return (
        loss / (2.0 * pairs),
        feature_grad(image_back, image_projection),
        feature_grad(text_back, text_projection),
        image_projection_grad,
        text_projection_grad,
    )


def solution(mesh):
    grid = Mesh(mesh.devices.reshape(2, 4, 2, 4, 2), ALL)
    rows = P(ALL, None)
    return jax.shard_map(
        body,
        mesh=grid,
        in_specs=(rows, rows, P(), P()),
        out_specs=(P(), rows, rows, P(), P()),
        check_vma=False,
    )
```

```python
import math

import jax
import jax.numpy as jnp
from jax import lax
from jax.experimental import pallas as pl
from jax.experimental.pallas import tpu as pltpu
from jax.sharding import Mesh, PartitionSpec as P

sharpness_factor = 100.0
norm_eps = 1e-06
X = ("xh", "xl")
PAIR_Z = ("xl", "z")
YZ = ("y", "z")
ALL = ("xh", "y", "xl", "z", "c")
TILE = 512
LOG2 = sharpness_factor * math.log2(math.e)
f32 = jnp.float32
bf16 = jnp.bfloat16


def normalize_rows(features, weight):
    projected = jnp.dot(features, weight, preferred_element_type=f32)
    radius = jnp.sqrt(jnp.sum(projected * projected, axis=1, keepdims=True) + norm_eps)
    return (projected / radius, radius)


def from_core(v):
    return lax.ppermute(v, "c", [(0, 1), (1, 0)])


def from_mirror(v):
    return lax.ppermute(v, X, [(i, 3 - i) for i in range(4)])


def from_x(v, k):
    return lax.ppermute(v, X, [(i, (i - k) % 4) for i in range(4)])


def from_y(v, k):
    return lax.ppermute(v, "y", [(i, (i - k) % 4) for i in range(4)])


def hbm(v):
    return pltpu.with_memory_space_constraint(v, pltpu.HBM)


def spread(v, axes, n):
    return lax.all_to_all(jnp.broadcast_to(v[None], (n,) + v.shape), axes, 0, 0)


def gather_text(pair):
    n = pair.shape[0] // 2
    up = from_y(pair, 1)
    down = from_y(pair, 3)
    far = [from_y(up[:n], 1), from_y(down[n:], 3)]
    return jnp.concatenate([pair, up] + far + [down], axis=0)


def column_totals(part):
    part = part.reshape(4, 2, -1)
    part = part + from_mirror(part)[:, ::-1]
    total = part
    for k in (1, 3, 2):
        total = total + jnp.roll(from_y(part, k), k, axis=0)
    return total.reshape(1, -1)


def row_totals(part):
    n = part.shape[1] // 2
    flipped = jnp.concatenate([part[:, n:], part[:, :n]], axis=1)

    def from_pair(v, xl, c):
        pairs = [(i, i ^ (2 * xl + c)) for i in range(4)]
        return lax.ppermute(v, ("xl", "c"), pairs)

    part = part + from_pair(part, 1, 0) + from_pair(flipped, 1, 1) + from_pair(flipped, 0, 1)
    return part + sum(lax.ppermute(part, "z", [(i, (i - k) % 4) for i in range(4)]) for k in (1, 3, 2))


def plus(*parts):
    return sum(p.astype(f32) for p in parts)


def scatter_text(g, image_part):
    b = g.shape[0] // 4
    h = b // 2
    g0, g1, g2, g3 = (g[k * b : (k + 1) * b] for k in range(4))
    low = from_y(g2[:h], 3)
    high = from_y(g2[h:], 1)
    g1 = jnp.concatenate([plus(g1[:h], low).astype(bf16), g1[h:]], axis=0)
    g3 = jnp.concatenate([g3[:h], plus(g3[h:], high).astype(bf16)], axis=0)
    g1, g3, image_part = lax.optimization_barrier((g1, g3, image_part))
    g0 = plus(g0, from_y(g1, 3), from_y(g3, 1))
    return g0[:h] + from_mirror(g0[h:].astype(bf16)).astype(f32), image_part


def params(mib=40):
    return pltpu.CompilerParams(vmem_limit_bytes=mib * 1024 * 1024)


def logits_kernel(mine, other, texts, logits, row_sum, column_sum):
    i = pl.program_id(0)
    images = jnp.where(i < pl.num_programs(0) // 2, mine[...], other[...])
    value = lax.dot_general(
        images, texts[...], (((1,), (1,)), ((), ())), preferred_element_type=f32
    )
    logits[...] = value
    e = jnp.exp2(value * LOG2 - LOG2)
    by_lane = e[:, :128]
    for k in range(1, e.shape[1] // 128):
        by_lane = by_lane + e[:, k * 128 : (k + 1) * 128]
    row_sum[...] = jnp.sum(by_lane.T, axis=0, keepdims=True)
    column_sum[...] = jnp.where(i == 0, 0.0, column_sum[...]) + jnp.sum(e, axis=0, keepdims=True)


def block_logits(mine, other, texts):
    rows, width = mine.shape
    n = 2 * rows
    m = texts.shape[0]
    steps = n // TILE
    half = steps // 2
    return pl.pallas_call(
        logits_kernel,
        grid=(steps,),
        in_specs=[
            pl.BlockSpec((TILE, width), lambda i: (jnp.minimum(i, half - 1), 0)),
            pl.BlockSpec((TILE, width), lambda i: (jnp.maximum(i - half, 0), 0)),
            pl.BlockSpec((m, width), lambda i: (0, 0)),
        ],
        out_specs=[
            pl.BlockSpec((TILE, m), lambda i: (i, 0)),
            pl.BlockSpec((1, TILE), lambda i: (0, i)),
            pl.BlockSpec((1, m), lambda i: (0, 0)),
        ],
        out_shape=[
            pltpu.HBM((n, m), f32),
            jax.ShapeDtypeStruct((1, n), f32),
            jax.ShapeDtypeStruct((1, m), f32),
        ],
        compiler_params=params(),
        cost_estimate=pl.CostEstimate(
            flops=2 * n * m * width, bytes_accessed=4 * n * m + 2 * (n + m) * width, transcendentals=n * m
        ),
        name="block_logits",
    )(mine, other, texts)


def grads_kernel(
    place, logits, row_total, column_total, mine, other, texts, own, part_mine, part_other, text_part, total, last
):
    i = pl.program_id(0)
    half = (pl.num_programs(0) - 1) // 2
    before = jnp.where(i == 0, jnp.zeros((), bf16), last[...])
    images = jnp.where(i <= half, mine[...], other[...])
    part = jnp.dot(before, texts[...], preferred_element_type=f32)
    share = lax.dot_general(
        before, images, (((0,), (0,)), ((), ())), preferred_element_type=f32
    )
    shift = LOG2 - math.log2(0.5 * sharpness_factor)
    value = logits[...] * LOG2
    rows, columns = value.shape
    row_lse = jnp.log2(row_total[...]) + shift
    column_lse = jnp.log2(column_total[...]) + shift
    by_row = jnp.broadcast_to(row_lse, (128, rows)).T
    by_row = jnp.concatenate([by_row] * (columns // 128), axis=1)
    last[...] = (jnp.exp2(value - by_row) + jnp.exp2(value - column_lse)).astype(bf16)
    total[...] = jnp.where(i == 0, 0.0, total[...]) + share
    per = rows // 128

    @pl.when(i <= half)
    def _():
        for k in range(per):
            here = jnp.where(place[0] == (i - 1) * per + k, sharpness_factor, 0.0)
            part_mine[k * 128 : (k + 1) * 128, :] = (
                part[k * 128 : (k + 1) * 128] - here * texts[:128, :].astype(f32)
            ).astype(bf16)

    @pl.when(i > half)
    def _():
        part_other[...] = part.astype(bf16)

    @pl.when(i == pl.num_programs(0) - 1)
    def _():
        text_part[:128, :] = (total[:128, :] - sharpness_factor * own[...].astype(f32)).astype(bf16)
        text_part[128:, :] = total[128:, :].astype(bf16)


def block_grads(place, logits, row_total, column_total, mine, other, texts, own):
    n, m = logits.shape
    width = texts.shape[1]
    steps = n // TILE
    half = steps // 2
    first = pl.BlockSpec((TILE, width), lambda i: (jnp.clip(i - 1, 0, half - 1), 0))
    second = pl.BlockSpec((TILE, width), lambda i: (jnp.clip(i - 1 - half, 0, half - 1), 0))
    return pl.pallas_call(
        grads_kernel,
        grid=(steps + 1,),
        in_specs=[
            pl.BlockSpec(memory_space=pltpu.SMEM),
            pl.BlockSpec((TILE, m), lambda i: (jnp.minimum(i, steps - 1), 0)),
            pl.BlockSpec((1, TILE), lambda i: (0, jnp.minimum(i, steps - 1))),
            pl.BlockSpec((1, m), lambda i: (0, 0)),
            first,
            second,
            pl.BlockSpec((m, width), lambda i: (0, 0)),
            pl.BlockSpec(own.shape, lambda i: (0, 0)),
        ],
        out_specs=[
            first,
            second,
            pl.BlockSpec((m, width), lambda i: (0, 0)),
        ],
        out_shape=[
            jax.ShapeDtypeStruct((n // 2, width), bf16),
            jax.ShapeDtypeStruct((n // 2, width), bf16),
            jax.ShapeDtypeStruct((m, width), bf16),
        ],
        scratch_shapes=[pltpu.VMEM((m, width), f32), pltpu.VMEM((TILE, m), bf16)],
        compiler_params=params(),
        cost_estimate=pl.CostEstimate(
            flops=4 * n * m * width,
            bytes_accessed=4 * n * m + 4 * (n + m) * width,
            transcendentals=2 * n * m,
        ),
        name="block_grads",
    )(place, logits, row_total, column_total, mine, other, texts, own)


def whole_kernel(core, mine, other, image, text):
    rows = image.shape[0] // mine.shape[0]

    def put(src):
        image[...] = src[:, :rows].astype(f32).reshape(image.shape)
        text[...] = src[:, rows:].astype(f32).reshape(text.shape)

    @pl.when(pl.program_id(0) == core[0])
    def _():
        put(mine)

    @pl.when(pl.program_id(0) != core[0])
    def _():
        put(other)


def whole_terms(core, mine, other, rows):
    n, both, width = mine.shape
    block = pl.BlockSpec(mine.shape, lambda h: (0, 0, 0))
    return pl.pallas_call(
        whole_kernel,
        grid=(2,),
        in_specs=[pl.BlockSpec(memory_space=pltpu.SMEM), block, block],
        out_specs=[
            pl.BlockSpec((n * rows, width), lambda h: (h, 0)),
            pl.BlockSpec((n * (both - rows), width), lambda h: (h, 0)),
        ],
        out_shape=[
            jax.ShapeDtypeStruct((2 * n * rows, width), f32),
            jax.ShapeDtypeStruct((2 * n * (both - rows), width), f32),
        ],
        compiler_params=params(),
        cost_estimate=pl.CostEstimate(flops=0, bytes_accessed=12 * n * both * width, transcendentals=0),
        name="whole_terms",
    )(core, mine, other)


def other_half(v, core):
    n = v.shape[1] // 2
    mine = lax.dynamic_slice_in_dim(v, core * n, n, axis=1)
    away = lax.dynamic_slice_in_dim(v, (1 - core) * n, n, axis=1)
    return jnp.concatenate([mine, from_core(away)], axis=0)


def back_rows(unit_rows, radius, emb_grad):
    along = jnp.sum(unit_rows * emb_grad, axis=1, keepdims=True)
    return ((emb_grad - unit_rows * along) / radius).astype(bf16)


def feature_grad(projected_grad, weight):
    return lax.dot_general(
        projected_grad, weight, (((1,), (1,)), ((), ())), preferred_element_type=f32
    ).astype(bf16)


def weight_grad(features, projected_grad):
    return lax.dot_general(
        features, projected_grad, (((0,), (0,)), ((), ())), preferred_element_type=f32
    )


def reduce_weights(image_term, text_term, loss_part, core):
    n = 16
    width = image_term.shape[1]
    image_blocks = image_term.astype(bf16).reshape(n, -1, width)
    text_blocks = text_term.astype(bf16).reshape(n, -1, width)
    rows = image_blocks.shape[1]
    both = rows + text_blocks.shape[1]
    lane = lax.broadcasted_iota(jnp.int32, (8, width), 1)

    def split(v):
        high = lax.reduce_precision(v, 8, 7)
        low = (v - high).astype(bf16)
        return jnp.where(lane == 0, high.astype(bf16), jnp.where(lane == 1, low, jnp.zeros((), bf16)))

    extra = jnp.broadcast_to(split(loss_part), (n, 8, width))
    sent = jnp.concatenate([image_blocks, text_blocks, extra], axis=1)
    got = plus(*lax.all_to_all(sent, YZ, 0, 0))
    block = jnp.concatenate(
        [got[:both].astype(bf16), split(got[both:, 0:1] + got[both:, 1:2])], axis=0
    )
    total = plus(block, *(from_x(block, k) for k in (1, 3, 2)))
    loss = total[both, 0] + total[both, 1]
    full = spread(total[:both].astype(bf16), YZ, n)
    image, text = whole_terms(core.reshape(1), full, from_core(full), rows)
    return image, text, loss


def body(image_features, text_features, image_projection, text_projection):
    core = lax.axis_index("c")
    place = lax.axis_index(PAIR_Z)
    text_unit, text_radius = normalize_rows(text_features, text_projection)
    text_emb = text_unit.astype(bf16)
    image_unit, image_radius = normalize_rows(image_features, image_projection)
    image_emb = image_unit.astype(bf16)
    own, width = image_emb.shape
    images = spread(image_emb, PAIR_Z, 8).reshape(8 * own, width)
    pair = jnp.concatenate([text_emb, from_mirror(text_emb)], axis=0)
    pair, later_image, later_text = lax.optimization_barrier((pair, image_features, text_features))
    image_halves = other_half(later_image, core)
    text_halves = other_half(later_text, core)
    images, texts, image_halves, text_halves = lax.optimization_barrier(
        (images, gather_text(pair), image_halves, text_halves)
    )
    images_other = hbm(from_core(images))
    texts = hbm(texts)
    logits, row_part, column_part = block_logits(images, images_other, texts)
    row_total = row_totals(row_part)
    column_total = column_totals(column_part)
    image_part, other_part, text_part = block_grads(
        place.reshape(1), logits, row_total, column_total, images, images_other, texts, image_emb
    )
    image_part = plus(image_part, from_core(other_part)).astype(bf16)
    text_emb_grad, image_part = scatter_text(text_part, image_part)
    image_emb_grad = plus(*lax.all_to_all(image_part.reshape(8, own, width), PAIR_Z, 0, 0))
    matched = sharpness_factor * jnp.sum(image_emb.astype(f32) * text_emb.astype(f32), axis=1)
    own_rows = lax.dynamic_slice_in_dim(row_total[0], place * own, own)
    loss_part = jnp.sum(
        jnp.log(own_rows)
        + jnp.log(column_total[0, :own])
        + 2.0 * (sharpness_factor - matched)
    )
    loss_part = loss_part + from_core(loss_part)
    text_back = back_rows(text_unit, text_radius, text_emb_grad)
    image_back = back_rows(image_unit, image_radius, image_emb_grad)
    text_both = jnp.concatenate([text_back, from_core(text_back)], axis=0)
    image_both = jnp.concatenate([image_back, from_core(image_back)], axis=0)
    text_term = weight_grad(text_halves, text_both)
    image_term = weight_grad(image_halves, image_both)
    image_projection_grad, text_projection_grad, loss = reduce_weights(
        image_term, text_term, loss_part, core
    )
    pairs = own * 128
    return (
        loss / (2.0 * pairs),
        feature_grad(image_back, image_projection),
        feature_grad(text_back, text_projection),
        image_projection_grad,
        text_projection_grad,
    )


def solution(mesh):
    grid = Mesh(mesh.devices.reshape(2, 4, 2, 4, 2), ALL)
    rows = P(ALL, None)
    return jax.shard_map(
        body,
        mesh=grid,
        in_specs=(rows, rows, P(), P()),
        out_specs=(P(), rows, rows, P(), P()),
        check_vma=False,
    )
```

```python
import math

import jax
import jax.numpy as jnp
from jax import lax
from jax.experimental import pallas as pl
from jax.experimental.pallas import tpu as pltpu
from jax.sharding import Mesh, PartitionSpec as P

sharpness_factor = 100.0
norm_eps = 1e-06
X = ("xh", "xl")
PAIR_Z = ("xl", "z")
YZ = ("y", "z")
ALL = ("xh", "y", "xl", "z", "c")
TILE = 512
LOG2 = sharpness_factor * math.log2(math.e)
f32 = jnp.float32
bf16 = jnp.bfloat16


def normalize_rows(features, weight):
    projected = jnp.dot(features, weight, preferred_element_type=f32)
    radius = jnp.sqrt(jnp.sum(projected * projected, axis=1, keepdims=True) + norm_eps)
    return (projected / radius, radius)


def from_core(v):
    return lax.ppermute(v, "c", [(0, 1), (1, 0)])


def from_mirror(v):
    return lax.ppermute(v, X, [(i, 3 - i) for i in range(4)])


def from_x(v, k):
    return lax.ppermute(v, X, [(i, (i - k) % 4) for i in range(4)])


def from_y(v, k):
    return lax.ppermute(v, "y", [(i, (i - k) % 4) for i in range(4)])


def hbm(v):
    return pltpu.with_memory_space_constraint(v, pltpu.HBM)


def spread(v, axes, n):
    return lax.all_to_all(jnp.broadcast_to(v[None], (n,) + v.shape), axes, 0, 0)


def gather_text(pair):
    n = pair.shape[0] // 2
    up = from_y(pair, 1)
    down = from_y(pair, 3)
    far = [from_y(up[:n], 1), from_y(down[n:], 3)]
    return jnp.concatenate([pair, up] + far + [down], axis=0)


def column_totals(part):
    part = part.reshape(4, 2, -1)
    part = part + from_mirror(part)[:, ::-1]
    total = part
    for k in (1, 3, 2):
        total = total + jnp.roll(from_y(part, k), k, axis=0)
    return total.reshape(1, -1)


def row_totals(part):
    n = part.shape[1] // 2
    flipped = jnp.concatenate([part[:, n:], part[:, :n]], axis=1)

    def from_pair(v, xl, c):
        pairs = [(i, i ^ (2 * xl + c)) for i in range(4)]
        return lax.ppermute(v, ("xl", "c"), pairs)

    part = part + from_pair(part, 1, 0) + from_pair(flipped, 1, 1) + from_pair(flipped, 0, 1)
    return part + sum(lax.ppermute(part, "z", [(i, (i - k) % 4) for i in range(4)]) for k in (1, 3, 2))


def plus(*parts):
    return sum(p.astype(f32) for p in parts)


def scatter_text(g, image_part):
    b = g.shape[0] // 4
    h = b // 2
    g0, g1, g2, g3 = (g[k * b : (k + 1) * b] for k in range(4))
    low = from_y(g2[:h], 3)
    high = from_y(g2[h:], 1)
    g1 = jnp.concatenate([plus(g1[:h], low).astype(bf16), g1[h:]], axis=0)
    g3 = jnp.concatenate([g3[:h], plus(g3[h:], high).astype(bf16)], axis=0)
    g1, g3, image_part = lax.optimization_barrier((g1, g3, image_part))
    g0 = plus(g0, from_y(g1, 3), from_y(g3, 1))
    return g0[:h] + from_mirror(g0[h:].astype(bf16)).astype(f32), image_part


def params(mib=40):
    return pltpu.CompilerParams(vmem_limit_bytes=mib * 1024 * 1024)


def logits_kernel(mine, other, texts, logits, row_sum, column_sum):
    i = pl.program_id(0)
    images = jnp.where(i < pl.num_programs(0) // 2, mine[...], other[...])
    value = lax.dot_general(
        images, texts[...], (((1,), (1,)), ((), ())), preferred_element_type=f32
    )
    logits[...] = value
    e = jnp.exp2(value * LOG2 - LOG2)
    by_lane = e[:, :128]
    for k in range(1, e.shape[1] // 128):
        by_lane = by_lane + e[:, k * 128 : (k + 1) * 128]
    row_sum[...] = jnp.sum(by_lane.T, axis=0, keepdims=True)
    column_sum[...] = jnp.where(i == 0, 0.0, column_sum[...]) + jnp.sum(e, axis=0, keepdims=True)


def block_logits(mine, other, texts):
    rows, width = mine.shape
    n = 2 * rows
    m = texts.shape[0]
    steps = n // TILE
    half = steps // 2
    return pl.pallas_call(
        logits_kernel,
        grid=(steps,),
        in_specs=[
            pl.BlockSpec((TILE, width), lambda i: (jnp.minimum(i, half - 1), 0)),
            pl.BlockSpec((TILE, width), lambda i: (jnp.maximum(i - half, 0), 0)),
            pl.BlockSpec((m, width), lambda i: (0, 0)),
        ],
        out_specs=[
            pl.BlockSpec((TILE, m), lambda i: (i, 0)),
            pl.BlockSpec((1, TILE), lambda i: (0, i)),
            pl.BlockSpec((1, m), lambda i: (0, 0)),
        ],
        out_shape=[
            pltpu.HBM((n, m), f32),
            jax.ShapeDtypeStruct((1, n), f32),
            jax.ShapeDtypeStruct((1, m), f32),
        ],
        compiler_params=params(),
        cost_estimate=pl.CostEstimate(
            flops=2 * n * m * width, bytes_accessed=4 * n * m + 2 * (n + m) * width, transcendentals=n * m
        ),
        name="block_logits",
    )(mine, other, texts)


def grads_kernel(
    place, logits, row_total, column_total, mine, other, texts, own, part_mine, part_other, text_part, total, last
):
    i = pl.program_id(0)
    half = (pl.num_programs(0) - 1) // 2
    before = jnp.where(i == 0, jnp.zeros((), bf16), last[...])
    images = jnp.where(i <= half, mine[...], other[...])
    part = jnp.dot(before, texts[...], preferred_element_type=f32)
    share = lax.dot_general(
        before, images, (((0,), (0,)), ((), ())), preferred_element_type=f32
    )
    shift = LOG2 - math.log2(0.5 * sharpness_factor)
    value = logits[...] * LOG2
    rows, columns = value.shape
    row_lse = jnp.log2(row_total[...]) + shift
    column_lse = jnp.log2(column_total[...]) + shift
    by_row = jnp.broadcast_to(row_lse, (128, rows)).T
    by_row = jnp.concatenate([by_row] * (columns // 128), axis=1)
    last[...] = (jnp.exp2(value - by_row) + jnp.exp2(value - column_lse)).astype(bf16)
    total[...] = jnp.where(i == 0, 0.0, total[...]) + share
    per = rows // 128

    @pl.when(i <= half)
    def _():
        for k in range(per):
            here = jnp.where(place[0] == (i - 1) * per + k, sharpness_factor, 0.0)
            part_mine[k * 128 : (k + 1) * 128, :] = (
                part[k * 128 : (k + 1) * 128] - here * texts[:128, :].astype(f32)
            ).astype(bf16)

    @pl.when(i > half)
    def _():
        part_other[...] = part.astype(bf16)

    @pl.when(i == pl.num_programs(0) - 1)
    def _():
        text_part[:128, :] = (total[:128, :] - sharpness_factor * own[...].astype(f32)).astype(bf16)
        text_part[128:, :] = total[128:, :].astype(bf16)


def block_grads(place, logits, row_total, column_total, mine, other, texts, own):
    n, m = logits.shape
    width = texts.shape[1]
    steps = n // TILE
    half = steps // 2
    first = pl.BlockSpec((TILE, width), lambda i: (jnp.clip(i - 1, 0, half - 1), 0))
    second = pl.BlockSpec((TILE, width), lambda i: (jnp.clip(i - 1 - half, 0, half - 1), 0))
    return pl.pallas_call(
        grads_kernel,
        grid=(steps + 1,),
        in_specs=[
            pl.BlockSpec(memory_space=pltpu.SMEM),
            pl.BlockSpec((TILE, m), lambda i: (jnp.minimum(i, steps - 1), 0)),
            pl.BlockSpec((1, TILE), lambda i: (0, jnp.minimum(i, steps - 1))),
            pl.BlockSpec((1, m), lambda i: (0, 0)),
            first,
            second,
            pl.BlockSpec((m, width), lambda i: (0, 0)),
            pl.BlockSpec(own.shape, lambda i: (0, 0)),
        ],
        out_specs=[
            first,
            second,
            pl.BlockSpec((m, width), lambda i: (0, 0)),
        ],
        out_shape=[
            jax.ShapeDtypeStruct((n // 2, width), bf16),
            jax.ShapeDtypeStruct((n // 2, width), bf16),
            jax.ShapeDtypeStruct((m, width), bf16),
        ],
        scratch_shapes=[pltpu.VMEM((m, width), f32), pltpu.VMEM((TILE, m), bf16)],
        compiler_params=params(),
        cost_estimate=pl.CostEstimate(
            flops=4 * n * m * width,
            bytes_accessed=4 * n * m + 4 * (n + m) * width,
            transcendentals=2 * n * m,
        ),
        name="block_grads",
    )(place, logits, row_total, column_total, mine, other, texts, own)


def whole_kernel(core, mine, other, image, text):
    rows = image.shape[0] // mine.shape[0]

    def put(src):
        image[...] = src[:, :rows].astype(f32).reshape(image.shape)
        text[...] = src[:, rows:].astype(f32).reshape(text.shape)

    @pl.when(pl.program_id(0) == core[0])
    def _():
        put(mine)

    @pl.when(pl.program_id(0) != core[0])
    def _():
        put(other)


def whole_terms(core, mine, other, rows):
    n, both, width = mine.shape
    block = pl.BlockSpec(mine.shape, lambda h: (0, 0, 0))
    return pl.pallas_call(
        whole_kernel,
        grid=(2,),
        in_specs=[pl.BlockSpec(memory_space=pltpu.SMEM), block, block],
        out_specs=[
            pl.BlockSpec((n * rows, width), lambda h: (h, 0)),
            pl.BlockSpec((n * (both - rows), width), lambda h: (h, 0)),
        ],
        out_shape=[
            jax.ShapeDtypeStruct((2 * n * rows, width), f32),
            jax.ShapeDtypeStruct((2 * n * (both - rows), width), f32),
        ],
        compiler_params=params(),
        cost_estimate=pl.CostEstimate(flops=0, bytes_accessed=12 * n * both * width, transcendentals=0),
        name="whole_terms",
    )(core, mine, other)


def other_half(v, core):
    n = v.shape[1] // 2
    mine = lax.dynamic_slice_in_dim(v, core * n, n, axis=1)
    away = lax.dynamic_slice_in_dim(v, (1 - core) * n, n, axis=1)
    return jnp.concatenate([mine, from_core(away)], axis=0)


def back_rows(unit_rows, radius, emb_grad):
    along = jnp.sum(unit_rows * emb_grad, axis=1, keepdims=True)
    return ((emb_grad - unit_rows * along) / radius).astype(bf16)


def feature_grad(projected_grad, weight):
    return lax.dot_general(
        projected_grad, weight, (((1,), (1,)), ((), ())), preferred_element_type=f32
    ).astype(bf16)


def weight_grad(features, projected_grad):
    return lax.dot_general(
        features, projected_grad, (((0,), (0,)), ((), ())), preferred_element_type=f32
    )


def reduce_weights(image_term, text_term, loss_part, core):
    n = 16
    width = image_term.shape[1]
    image_blocks = image_term.astype(bf16).reshape(n, -1, width)
    text_blocks = text_term.astype(bf16).reshape(n, -1, width)
    rows = image_blocks.shape[1]
    both = rows + text_blocks.shape[1]
    lane = lax.broadcasted_iota(jnp.int32, (8, width), 1)

    def split(v):
        high = lax.reduce_precision(v, 8, 7)
        low = (v - high).astype(bf16)
        return jnp.where(lane == 0, high.astype(bf16), jnp.where(lane == 1, low, jnp.zeros((), bf16)))

    extra = jnp.broadcast_to(split(loss_part), (n, 8, width))
    sent = jnp.concatenate([image_blocks, text_blocks, extra], axis=1)
    got = plus(*lax.all_to_all(sent, YZ, 0, 0))
    block = jnp.concatenate(
        [got[:both].astype(bf16), split(got[both:, 0:1] + got[both:, 1:2])], axis=0
    )
    total = plus(block, *(from_x(block, k) for k in (1, 3, 2)))
    loss = total[both, 0] + total[both, 1]
    full = spread(total[:both].astype(bf16), YZ, n)
    image, text = whole_terms(core.reshape(1), full, from_core(full), rows)
    return image, text, loss


def body(image_features, text_features, image_projection, text_projection):
    core = lax.axis_index("c")
    place = lax.axis_index(PAIR_Z)
    text_unit, text_radius = normalize_rows(text_features, text_projection)
    text_emb = text_unit.astype(bf16)
    image_unit, image_radius = normalize_rows(image_features, image_projection)
    image_emb = image_unit.astype(bf16)
    own, width = image_emb.shape
    images = spread(image_emb, PAIR_Z, 8).reshape(8 * own, width)
    pair = jnp.concatenate([text_emb, from_mirror(text_emb)], axis=0)
    pair, later_image, later_text = lax.optimization_barrier((pair, image_features, text_features))
    image_halves = other_half(later_image, core)
    text_halves = other_half(later_text, core)
    images, texts, image_halves, text_halves = lax.optimization_barrier(
        (images, gather_text(pair), image_halves, text_halves)
    )
    images_other = hbm(from_core(images))
    logits, row_part, column_part = block_logits(images, images_other, texts)
    row_total = row_totals(row_part)
    column_total = column_totals(column_part)
    image_part, other_part, text_part = block_grads(
        place.reshape(1), logits, row_total, column_total, images, images_other, texts, image_emb
    )
    image_part = plus(image_part, from_core(other_part)).astype(bf16)
    text_emb_grad, image_part = scatter_text(text_part, image_part)
    image_emb_grad = plus(*lax.all_to_all(image_part.reshape(8, own, width), PAIR_Z, 0, 0))
    matched = sharpness_factor * jnp.sum(image_emb.astype(f32) * text_emb.astype(f32), axis=1)
    own_rows = lax.dynamic_slice_in_dim(row_total[0], place * own, own)
    loss_part = jnp.sum(
        jnp.log(own_rows)
        + jnp.log(column_total[0, :own])
        + 2.0 * (sharpness_factor - matched)
    )
    loss_part = loss_part + from_core(loss_part)
    text_back = back_rows(text_unit, text_radius, text_emb_grad)
    image_back = back_rows(image_unit, image_radius, image_emb_grad)
    text_both = jnp.concatenate([text_back, from_core(text_back)], axis=0)
    image_both = jnp.concatenate([image_back, from_core(image_back)], axis=0)
    text_term = weight_grad(text_halves, text_both)
    image_term = weight_grad(image_halves, image_both)
    image_projection_grad, text_projection_grad, loss = reduce_weights(
        image_term, text_term, loss_part, core
    )
    pairs = own * 128
    return (
        loss / (2.0 * pairs),
        feature_grad(image_back, image_projection),
        feature_grad(text_back, text_projection),
        image_projection_grad,
        text_projection_grad,
    )


def solution(mesh):
    grid = Mesh(mesh.devices.reshape(2, 4, 2, 4, 2), ALL)
    rows = P(ALL, None)
    return jax.shard_map(
        body,
        mesh=grid,
        in_specs=(rows, rows, P(), P()),
        out_specs=(P(), rows, rows, P(), P()),
        check_vma=False,
    )
```
